768 devices in a mesh: occ: 24 (over z, x_hi), vir: 32 (over x_lo, y, core).
Axes of the slice: x: 4 (x_hi: 2, x_lo: 2; x = x_hi * 2 + x_lo), y: 8, z: 12, core: 2. Of those that a mesh axis runs over, the one named last changes fastest.
Arguments:
- integrals: float32 [24, 768, 1536], P(None, 'vir', 'occ'), may hold values from -1.5 to 1.5
- occ_bins: int32 [24], replicated, may hold values from 0 to 99
- vir_bins: int32 [768], replicated, may hold values from 0 to 299
Outputs:
- density: float32 [768, 24, 1536], P('vir', 'occ')
The draws below stay inside these ranges and needn't reach their ends.
All inputs are finite; a program needn't handle non-finite values.
Results may differ from the reference program's by a relative error of at most 0.0032.
Values may be sent and summed in bfloat16 or wider, within the bound.
No kernel may reach another device: no remote copies, remote signals or barrier semaphores. Data moves between devices by JAX's collectives and lax.ppermute only.
A program may use at most 32 MiB of HBM per device.

```python
import jax
import jax.numpy as jnp
from jax import lax

V = 768
X = 1536
NO = 24


def plant(drawn, stream_key, smallest, high):
    spot = [jax.random.randint(jax.random.fold_in(stream_key, axis), (), 0, length) for axis, length in enumerate(drawn.shape)]
    widest = drawn.shape.index(max(drawn.shape))
    next_to = spot[:widest] + [(spot[widest] + 1) % drawn.shape[widest]] + spot[widest + 1:]
    return drawn.at[tuple(spot)].set(smallest).at[tuple(next_to)].set(high)


def levels(stream_key, shape, split, least, top_value):
    gain = 1.0
    for position, shards_of in split:
        steps = jax.random.uniform(jax.random.fold_in(jax.random.fold_in(stream_key, 6), position), (shards_of,), jnp.float32, least / len(split), top_value / len(split))
        gain = gain * jnp.repeat(jnp.exp(steps), shape[position] // shards_of).reshape((-1,) + (1,) * (len(shape) - 1 - position))
    return gain


def bell_draw(rng, shape, deviation, most, split=(), kind=jnp.bfloat16):
    loudness = levels(rng, shape, split, -0.22, 0.18) if split else 1.0
    values = jax.random.normal(rng, shape, jnp.float32) * deviation * loudness
    return jnp.minimum(jnp.maximum(values, -most), most).astype(kind)


def setup_inputs(seed: int = 0) -> dict:
    keys = jax.random.split(jax.random.key(seed), 4)
    integrals = bell_draw(keys[0], (NO, V, X), (1.7 / (X * NO * V) ** 0.1667), 1.5, ((1, 32), (2, 24)), jnp.float32)
    occ_bins = plant(jax.random.randint(keys[1], (NO,), 0, 100), jax.random.fold_in(keys[1], 1), 0, 99).astype(jnp.int32)
    vir_bins = plant(jax.random.randint(keys[2], (V,), 0, 300), jax.random.fold_in(keys[2], 1), 0, 299).astype(jnp.int32)
    return {"integrals": integrals, "occ_bins": occ_bins, "vir_bins": vir_bins}


occupied_base = -0.4
occupied_step = 0.01
virtual_base = 0.1
virtual_step = 0.01
spin_scale = 1.3


def reference(integrals, occ_bins, vir_bins):
    rounded = lax.optimization_barrier(integrals.astype(jnp.bfloat16)).astype(jnp.float32)
    occupied = occupied_base - occupied_step * occ_bins.astype(jnp.float32)
    virtual = virtual_base + virtual_step * vir_bins.astype(jnp.float32)

    def one_occupied(orbital):
        orbital_rows = lax.dynamic_index_in_dim(rounded, orbital, 0, keepdims=False)
        pair_values = jnp.einsum('ap,jbp->ajb', orbital_rows, rounded, precision=lax.Precision.HIGHEST)
        occ_here = lax.dynamic_index_in_dim(occupied, orbital, 0, keepdims=False)
        denominator = virtual[:, None, None] + virtual[None, None, :] - occ_here - occupied[None, :, None]
        amplitude = (spin_scale * pair_values / denominator).astype(jnp.bfloat16)
        amplitude = lax.optimization_barrier(amplitude).astype(jnp.float32)
        return jnp.einsum('ajb,jbp->ap', amplitude, rounded, precision=lax.Precision.HIGHEST)

    density = lax.map(one_occupied, jnp.arange(NO, dtype=jnp.int32))
    return jnp.transpose(density, (1, 0, 2))
```

```python
import jax
import jax.numpy as jnp
from jax import lax
from jax.experimental import pallas as pl
from jax.experimental.pallas import tpu as pltpu
from jax.sharding import Mesh, PartitionSpec as P

occupied_base = -0.4
occupied_step = 0.01
virtual_base = 0.1
virtual_step = 0.01
spin_scale = 1.3

SWAP = [(0, 1), (1, 0)]


def half_kernel(chunks, more, *refs):
    if more:
        rows_ref, cols_ref, row_e, col_e, before_ref, out_ref, full, sem = refs
    else:
        rows_ref, cols_ref, row_e, col_e, out_ref, full, sem = refs
    copies = []
    for k in range(chunks):
        copies.append(
            pltpu.make_async_copy(cols_ref.at[k], full.at[:, pl.ds(k * 128, 128)], sem.at[k])
        )
    for copy in copies:
        copy.start()
    for copy in copies:
        copy.wait()
    held = full[...]
    pair = lax.dot_general(
        rows_ref[...], held, (((1,), (1,)), ((), ())), preferred_element_type=jnp.float32
    )
    amplitude = (spin_scale * pair / (row_e[...] + col_e[...])).astype(jnp.bfloat16)
    term = jnp.dot(amplitude, held, preferred_element_type=jnp.float32)
    if more:
        term = term + before_ref[...]
    out_ref[...] = term.astype(out_ref.dtype)


def half(rows, cols, row_e, col_e, before=None):
    chunks, width, _ = cols.shape
    height, depth = rows.shape
    more = before is not None
    vmem = pl.BlockSpec(memory_space=pltpu.VMEM)
    ins = [rows, cols, row_e, col_e] + ([before] if more else [])
    specs = [vmem, pl.BlockSpec(memory_space=pl.ANY), vmem, vmem] + ([vmem] if more else [])

    def body(*refs):
        half_kernel(chunks, more, *refs)

    return pl.pallas_call(
        body,
        out_shape=jax.ShapeDtypeStruct((height, depth), jnp.bfloat16 if more else jnp.float32),
        in_specs=specs,
        out_specs=vmem,
        scratch_shapes=[
            pltpu.VMEM((width, depth), jnp.bfloat16),
            pltpu.SemaphoreType.DMA((chunks,)),
        ],
        compiler_params=pltpu.CompilerParams(vmem_limit_bytes=24 * 1024 * 1024),
        cost_estimate=pl.CostEstimate(
            flops=4 * height * width * depth, bytes_accessed=2 * depth * (2 * height + width), transcendentals=0
        ),
    )(*ins)


def shards(integrals, occ_bins, vir_bins):
    nz, nh, nl, ny = (lax.axis_size(k) for k in ("z", "h", "l", "y"))
    z, h, l, y, c = (lax.axis_index(k) for k in ("z", "h", "l", "y", "c"))
    nj, slab, part = integrals.shape
    own = integrals.astype(jnp.bfloat16)
    packed = jnp.concatenate([own[: nj // 2], own[nj // 2 :]], axis=2)
    there = lax.ppermute(packed, "h", SWAP)
    other = jnp.concatenate([there[:, :, :part], there[:, :, part:]], axis=0)
    first = h == 0
    wide = jnp.concatenate([jnp.where(first, own, other), jnp.where(first, other, own)], axis=2)
    cols = lax.all_gather(wide.reshape(nj * slab, 2 * part), "z", axis=0, tiled=False)
    seeds = lax.dynamic_index_in_dim(wide.reshape(nz, nh, slab, 2 * part), h, 1, keepdims=False)
    seeds = lax.all_to_all(seeds, "z", 0, 0)
    seeds = jnp.transpose(seeds, (1, 0, 2)).reshape(slab, nz * 2 * part)
    rows = lax.all_to_all(
        jnp.broadcast_to(seeds[None], (nl * ny,) + seeds.shape), ("l", "y"), 0, 0
    ).reshape(nl * ny * slab, nz * 2 * part)
    cols, rows = lax.optimization_barrier((cols, rows))
    cols_there = lax.ppermute(cols, "c", SWAP)

    occupied = occupied_base - occupied_step * occ_bins.astype(jnp.float32)
    virtual = virtual_base + virtual_step * vir_bins.astype(jnp.float32)
    virtual = virtual.reshape(nl * ny, 2, slab)
    occ_own = lax.dynamic_index_in_dim(occupied, z * nh + h, 0, keepdims=False)
    row_e = (lax.dynamic_index_in_dim(virtual, c, 1, keepdims=False) - occ_own).reshape(-1, 1)
    here = lax.dynamic_index_in_dim(virtual, l * ny + y, 0, keepdims=False)
    col_own = lax.dynamic_index_in_dim(here, c, 0, keepdims=False)
    col_there = lax.dynamic_index_in_dim(here, 1 - c, 0, keepdims=False)
    col_own = (col_own[None, :] - occupied[:, None]).reshape(1, -1)
    col_there = (col_there[None, :] - occupied[:, None]).reshape(1, -1)

    before = half(rows, cols, row_e, col_own)
    partial_term = half(rows, cols_there, row_e, col_there, before)
    shares = lax.all_to_all(
        partial_term.reshape(nl * ny, slab, nz * 2 * part), ("l", "y"), 0, 0
    )
    density = jnp.sum(shares.astype(jnp.float32), axis=0)
    return density[:, None, :]


def solution(mesh):
    fine = Mesh(mesh.devices.reshape(12, 2, 2, 8, 2), ("z", "h", "l", "y", "c"))
    in_specs = (P(None, ("l", "y", "c"), ("z", "h")), P(), P())
    out_specs = P(("l", "y", "c"), ("z", "h"), None)
    return jax.shard_map(shards, mesh=fine, in_specs=in_specs, out_specs=out_specs, check_vma=False)
```

```python
import jax
import jax.numpy as jnp
from jax import lax
from jax.experimental import pallas as pl
from jax.experimental.pallas import tpu as pltpu
from jax.sharding import Mesh, PartitionSpec as P

occupied_base = -0.4
occupied_step = 0.01
virtual_base = 0.1
virtual_step = 0.01
spin_scale = 1.3

SWAP = [(0, 1), (1, 0)]


def load(cols_ref, full, sem):
    chunks = cols_ref.shape[0]
    copies = [
        pltpu.make_async_copy(cols_ref.at[k], full.at[:, pl.ds(k * 128, 128)], sem.at[k])
        for k in range(chunks)
    ]
    for copy in copies:
        copy.start()
    for copy in copies:
        copy.wait()


def term(rows, held, row_e, col_e):
    pair = lax.dot_general(
        rows, held, (((1,), (1,)), ((), ())), preferred_element_type=jnp.float32
    )
    amplitude = (spin_scale * pair / (row_e + col_e)).astype(jnp.bfloat16)
    return jnp.dot(amplitude, held, preferred_element_type=jnp.float32)


def both_kernel(cols_ref, col_e, there_ref, there_e, own_ref, own_e, there_out, own_out, full, sem):
    load(cols_ref, full, sem)
    there_out[...] = term(there_ref[...], full[...], there_e[...], col_e[...])
    own_out[...] = term(own_ref[...], full[...], own_e[...], col_e[...])


def add_kernel(cols_ref, col_e, rows_ref, row_e, before_ref, out_ref, full, sem):
    load(cols_ref, full, sem)
    total = before_ref[...] + term(rows_ref[...], full[...], row_e[...], col_e[...])
    out_ref[...] = total.astype(out_ref.dtype)


def run(kernel, cols, args, outs, space):
    chunks, width, lanes = cols.shape
    depth = chunks * lanes
    vmem = pl.BlockSpec(memory_space=pltpu.VMEM)
    work = 4 * sum(o.shape[0] for o in outs) * width * depth
    return pl.pallas_call(
        kernel,
        out_shape=outs,
        in_specs=[pl.BlockSpec(memory_space=space)] + [vmem] * len(args),
        out_specs=[vmem] * len(outs),
        scratch_shapes=[
            pltpu.VMEM((width, depth), jnp.bfloat16),
            pltpu.SemaphoreType.DMA((chunks,)),
        ],
        compiler_params=pltpu.CompilerParams(vmem_limit_bytes=24 * 1024 * 1024),
        cost_estimate=pl.CostEstimate(flops=work, bytes_accessed=4 * width * depth, transcendentals=0),
    )(cols, *args)


def shards(integrals, occ_bins, vir_bins):
    nz, nh, nl, ny = (lax.axis_size(k) for k in ("z", "h", "l", "y"))
    z, h, l, y, c = (lax.axis_index(k) for k in ("z", "h", "l", "y", "c"))
    nj, slab, part = integrals.shape
    depth = nz * nh * part
    own = integrals.astype(jnp.bfloat16)
    packed = jnp.concatenate([own[: nj // 2], own[nj // 2 :]], axis=2)
    there = lax.ppermute(packed, "h", SWAP)
    other = jnp.concatenate([there[:, :, :part], there[:, :, part:]], axis=0)
    first = h == 0
    wide = jnp.concatenate([jnp.where(first, own, other), jnp.where(first, other, own)], axis=2)
    cols = lax.all_gather(wide.reshape(nj * slab, nh * part), "z", axis=0, tiled=False)
    seeds = lax.dynamic_index_in_dim(wide.reshape(nz, nh, slab, nh * part), h, 1, keepdims=False)
    seeds = lax.all_to_all(seeds, "z", 0, 0)
    seeds = jnp.transpose(seeds, (1, 0, 2)).reshape(slab, depth)

    occupied = occupied_base - occupied_step * occ_bins.astype(jnp.float32)
    virtual = virtual_base + virtual_step * vir_bins.astype(jnp.float32)
    virtual = virtual.reshape(nl, ny, 2, slab)
    occ_own = lax.dynamic_index_in_dim(occupied, z * nh + h, 0, keepdims=False)
    of_core = lax.dynamic_index_in_dim(virtual, c, 2, keepdims=False) - occ_own
    own_e = lax.dynamic_index_in_dim(of_core, l, 0, keepdims=False).reshape(-1, 1)
    there_e = lax.dynamic_index_in_dim(of_core, 1 - l, 0, keepdims=False).reshape(-1, 1)
    of_chip = lax.dynamic_index_in_dim(virtual.reshape(nl * ny, 2, slab), l * ny + y, 0, keepdims=False)
    col_own = lax.dynamic_index_in_dim(of_chip, c, 0, keepdims=False)
    col_there = lax.dynamic_index_in_dim(of_chip, 1 - c, 0, keepdims=False)
    col_own = (col_own[None, :] - occupied[:, None]).reshape(1, -1)
    col_there = (col_there[None, :] - occupied[:, None]).reshape(1, -1)
    seeds, own_e, there_e, col_own, col_there = lax.optimization_barrier(
        (seeds, own_e, there_e, col_own, col_there)
    )

    rows_own = lax.all_to_all(jnp.broadcast_to(seeds[None], (ny, slab, depth)), "y", 0, 0)
    rows_own = rows_own.reshape(ny * slab, depth)
    rows_there = lax.ppermute(rows_own, "l", SWAP)
    cols, rows_own, rows_there = lax.optimization_barrier((cols, rows_own, rows_there))
    cols_there = lax.ppermute(cols, "c", SWAP)

    share = jax.ShapeDtypeStruct(rows_own.shape, jnp.float32)
    sent = jax.ShapeDtypeStruct(rows_own.shape, jnp.bfloat16)
    for_there, for_own = run(
        both_kernel, cols, (col_own, rows_there, there_e, rows_own, own_e), [share, share], pltpu.HBM
    )
    (for_there,) = run(
        add_kernel, cols_there, (col_there, rows_there, there_e, for_there), [sent], pl.ANY
    )
    arrived = lax.ppermute(for_there, "l", SWAP)
    (for_own,) = run(
        add_kernel, cols_there, (col_there, rows_own, own_e, for_own), [share], pl.ANY
    )
    pair_sum = (for_own + arrived.astype(jnp.float32)).astype(jnp.bfloat16)
    shares = lax.all_to_all(pair_sum.reshape(ny, slab, depth), "y", 0, 0)
    density = jnp.sum(shares.astype(jnp.float32), axis=0)
    return density[:, None, :]


def solution(mesh):
    fine = Mesh(mesh.devices.reshape(12, 2, 2, 8, 2), ("z", "h", "l", "y", "c"))
    in_specs = (P(None, ("l", "y", "c"), ("z", "h")), P(), P())
    out_specs = P(("l", "y", "c"), ("z", "h"), None)
    return jax.shard_map(shards, mesh=fine, in_specs=in_specs, out_specs=out_specs, check_vma=False)
```

```python
import jax
import jax.numpy as jnp
from jax import lax
from jax.experimental import pallas as pl
from jax.experimental.pallas import tpu as pltpu
from jax.sharding import Mesh, PartitionSpec as P

occupied_base = -0.4
occupied_step = 0.01
virtual_base = 0.1
virtual_step = 0.01
spin_scale = 1.3

SWAP = [(0, 1), (1, 0)]


def density_kernel(places, nz, rows_ref, row_e, col_e, *refs):
    blocks, (out_ref, full, sem) = refs[:-3], refs[-3:]
    width = full.shape[0] // 2
    z, c = lax.axis_index("z"), lax.axis_index("c")
    sign = 1 - 2 * c
    copies = []
    for block, parts in zip(blocks, places):
        for first, slab, steps in parts:
            place = pl.multiple_of(lax.rem(z + sign * steps + nz, nz) * 128, 128)
            half = slab if isinstance(slab, int) else (c if slab == "c" else 1 - c)
            copies.append(
                pltpu.make_async_copy(
                    block.at[pl.ds(first, width)],
                    full.at[pl.ds(pl.multiple_of(half * width, width), width), pl.ds(place, 128)],
                    sem.at[len(copies)],
                )
            )
    for copy in copies:
        copy.start()
    for copy in copies:
        copy.wait()
    for first in range(0, full.shape[0], width):
        held = full[first : first + width]
        pair = lax.dot_general(
            rows_ref[...], held, (((1,), (1,)), ((), ())), preferred_element_type=jnp.float32
        )
        amplitude = spin_scale * pair / (row_e[...] + col_e[:, first : first + width])
        term = jnp.dot(amplitude.astype(jnp.bfloat16), held, preferred_element_type=jnp.float32)
        total = term if first == 0 else total + term
    out_ref[...] = total.astype(out_ref.dtype)


def shards(integrals, occ_bins, vir_bins):
    nz, nh, nl, ny = (lax.axis_size(k) for k in ("z", "h", "l", "y"))
    z, h, l, y, c = (lax.axis_index(k) for k in ("z", "h", "l", "y", "c"))
    nj, slab, part = integrals.shape
    depth = nz * nh * part
    width = nj * slab
    own = integrals.astype(jnp.bfloat16)
    packed = jnp.concatenate([own[: nj // 2], own[nj // 2 :]], axis=2)
    there = lax.ppermute(packed, "h", SWAP)
    other = jnp.concatenate([there[:, :, :part], there[:, :, part:]], axis=0)
    first = h == 0
    wide = jnp.concatenate([jnp.where(first, own, other), jnp.where(first, other, own)], axis=2)
    wide = wide.reshape(width, nh * part)
    seeds = lax.all_to_all(own, ("z", "h"), 0, 0)
    wide_there = lax.ppermute(wide, "c", SWAP)
    lead = c == 0
    block = jnp.concatenate(
        [jnp.where(lead, wide, wide_there), jnp.where(lead, wide_there, wide)], axis=0
    )
    ring = [(2 * k, 2 * ((k + 1) % nz)) for k in range(nz)]
    ring += [(2 * k + 1, 2 * ((k + nz - 1) % nz) + 1) for k in range(nz)]
    steps = nz // 2
    step_one, seeds = lax.optimization_barrier((lax.ppermute(block, ("z", "c"), ring), seeds))
    blocks = [block, step_one]
    for _ in range(steps - 2):
        blocks.append(lax.ppermute(blocks[-1], ("z", "c"), ring))
    seeds = jnp.transpose(seeds, (1, 0, 2)).reshape(slab, depth)
    rows = lax.all_to_all(jnp.broadcast_to(seeds[None], (nl * ny, slab, depth)), ("l", "y"), 0, 0)
    rows = rows.reshape(nl * ny * slab, depth)
    mine = lax.dynamic_slice_in_dim(blocks[-1], c * width, width, 0)
    last = lax.ppermute(mine, ("z", "c"), ring)
    early = jnp.concatenate(blocks[1:4], axis=0)
    late = jnp.concatenate(blocks[4:] + [last], axis=0)
    early_there = lax.ppermute(early, "c", SWAP)
    late_there = lax.ppermute(late, "c", SWAP)

    occupied = occupied_base - occupied_step * occ_bins.astype(jnp.float32)
    virtual = virtual_base + virtual_step * vir_bins.astype(jnp.float32)
    virtual = virtual.reshape(nl * ny, 2, slab)
    occ_own = lax.dynamic_index_in_dim(occupied, z * nh + h, 0, keepdims=False)
    row_e = (lax.dynamic_index_in_dim(virtual, c, 1, keepdims=False) - occ_own).reshape(-1, 1)
    of_chip = lax.dynamic_index_in_dim(virtual, l * ny + y, 0, keepdims=False)
    col_e = (of_chip[:, None, :] - occupied[None, :, None]).reshape(1, -1)

    def whole(at, ahead):
        return [(at, 0, ahead), (at + width, 1, ahead)]

    places = [whole(0, -k) for k in range(steps)]
    places.append([(0, "c", steps)])
    places.append(sum([whole(2 * width * k, k + 1) for k in range(3)], []))
    rest = steps - 4
    places.append(
        sum([whole(2 * width * k, k + 4) for k in range(rest)], []) + [(2 * width * rest, "d", steps)]
    )

    vmem = pl.BlockSpec(memory_space=pltpu.VMEM)
    hbm = pl.BlockSpec(memory_space=pl.ANY)
    held = blocks + [last, early_there, late_there]
    partial_term = pl.pallas_call(
        lambda *refs: density_kernel(places, nz, *refs),
        out_shape=jax.ShapeDtypeStruct(rows.shape, jnp.bfloat16),
        in_specs=[vmem, vmem, vmem] + [hbm] * len(held),
        out_specs=vmem,
        scratch_shapes=[
            pltpu.VMEM((2 * width, depth), jnp.bfloat16),
            pltpu.SemaphoreType.DMA((2 * nz,)),
        ],
        compiler_params=pltpu.CompilerParams(vmem_limit_bytes=32 * 1024 * 1024),
        cost_estimate=pl.CostEstimate(
            flops=8 * rows.shape[0] * width * depth, bytes_accessed=4 * width * depth, transcendentals=0
        ),
    )(rows, row_e, col_e, *held)
    shares = lax.all_to_all(partial_term.reshape(nl * ny, slab, depth), ("l", "y"), 0, 0)
    density = jnp.sum(shares.astype(jnp.float32), axis=0)
    return density[:, None, :]


def solution(mesh):
    fine = Mesh(mesh.devices.reshape(12, 2, 2, 8, 2), ("z", "h", "l", "y", "c"))
    in_specs = (P(None, ("l", "y", "c"), ("z", "h")), P(), P())
    out_specs = P(("l", "y", "c"), ("z", "h"), None)
    return jax.shard_map(shards, mesh=fine, in_specs=in_specs, out_specs=out_specs, check_vma=False)
```

```python
import jax
import jax.numpy as jnp
from jax import lax
from jax.experimental import pallas as pl
from jax.experimental.pallas import tpu as pltpu
from jax.sharding import Mesh, PartitionSpec as P

occupied_base = -0.4
occupied_step = 0.01
virtual_base = 0.1
virtual_step = 0.01
spin_scale = 1.3

SWAP = [(0, 1), (1, 0)]


def load(cols_refs, full, sem):
    copies = []
    for n, cols_ref in enumerate(cols_refs):
        chunks, width, lanes = cols_ref.shape
        for k in range(chunks):
            place = full.at[pl.ds(n * width, width), pl.ds(k * lanes, lanes)]
            copies.append(pltpu.make_async_copy(cols_ref.at[k], place, sem.at[n, k]))
    for copy in copies:
        copy.start()
    for copy in copies:
        copy.wait()


def density_kernel(blocks, more, rows_ref, row_e, col_e, *refs):
    cols_refs, refs = refs[:blocks], refs[blocks:]
    before_ref = refs[0] if more else None
    out_ref, full, sem = refs[-3:]
    load(cols_refs, full, sem)
    pair = lax.dot_general(
        rows_ref[...], full[...], (((1,), (1,)), ((), ())), preferred_element_type=jnp.float32
    )
    amplitude = (spin_scale * pair / (row_e[...] + col_e[...])).astype(jnp.bfloat16)
    term = jnp.dot(amplitude, full[...], preferred_element_type=jnp.float32)
    if more:
        term = term + before_ref[...]
    out_ref[...] = term.astype(out_ref.dtype)


def run(rows, row_e, col_e, cols, before=None):
    chunks, width, lanes = cols[0].shape
    blocks, more = len(cols), before is not None
    vmem = pl.BlockSpec(memory_space=pltpu.VMEM)
    anywhere = pl.BlockSpec(memory_space=pl.ANY)
    work = 4 * rows.shape[0] * blocks * width * chunks * lanes
    return pl.pallas_call(
        lambda *refs: density_kernel(blocks, more, *refs),
        out_shape=jax.ShapeDtypeStruct(rows.shape, jnp.bfloat16 if more else jnp.float32),
        in_specs=[vmem] * 3 + [anywhere] * blocks + [vmem] * more,
        out_specs=vmem,
        scratch_shapes=[
            pltpu.VMEM((blocks * width, chunks * lanes), jnp.bfloat16),
            pltpu.SemaphoreType.DMA((blocks, chunks)),
        ],
        compiler_params=pltpu.CompilerParams(vmem_limit_bytes=24 * 1024 * 1024),
        cost_estimate=pl.CostEstimate(flops=work, bytes_accessed=work // 256, transcendentals=0),
    )(rows, row_e, col_e, *cols, *([before] if more else []))


def shards(integrals, occ_bins, vir_bins):
    nz, nh, nl, ny = (lax.axis_size(k) for k in ("z", "h", "l", "y"))
    z, h, l, y, c = (lax.axis_index(k) for k in ("z", "h", "l", "y", "c"))
    nj, slab, part = integrals.shape
    depth = nz * nh * part
    own = integrals.astype(jnp.bfloat16)
    packed = jnp.concatenate([own[: nj // 2], own[nj // 2 :]], axis=2)
    there = lax.ppermute(packed, "h", SWAP)
    other = jnp.concatenate([there[:, :, :part], there[:, :, part:]], axis=0)
    first = h == 0
    wide = jnp.concatenate([jnp.where(first, own, other), jnp.where(first, other, own)], axis=2)
    early = wide[: nj // 2].reshape(nj // 2 * slab, nh * part)
    late = wide[nj // 2 :].reshape(nj // 2 * slab, nh * part)
    seeds = lax.dynamic_index_in_dim(wide.reshape(nz, nh, slab, nh * part), h, 1, keepdims=False)
    seeds = lax.all_to_all(seeds, "z", 0, 0)
    cols_early = lax.all_gather(early, "z", axis=0, tiled=False)
    cols_early, seeds = lax.optimization_barrier((cols_early, seeds))
    seeds = jnp.transpose(seeds, (1, 0, 2)).reshape(slab, depth)
    seeds = jnp.broadcast_to(seeds[None], (nl * ny, slab, depth))
    late, seeds = lax.optimization_barrier((late, seeds))
    cols_late = lax.all_gather(late, "z", axis=0, tiled=False)
    rows = lax.all_to_all(seeds, ("l", "y"), 0, 0).reshape(nl * ny * slab, depth)
    early_there = lax.ppermute(cols_early, "c", SWAP)
    late_there = lax.ppermute(cols_late, "c", SWAP)

    occupied = occupied_base - occupied_step * occ_bins.astype(jnp.float32)
    virtual = virtual_base + virtual_step * vir_bins.astype(jnp.float32)
    virtual = virtual.reshape(nl * ny, 2, slab)
    occ_own = lax.dynamic_index_in_dim(occupied, z * nh + h, 0, keepdims=False)
    row_e = (lax.dynamic_index_in_dim(virtual, c, 1, keepdims=False) - occ_own).reshape(-1, 1)
    of_chip = lax.dynamic_index_in_dim(virtual, l * ny + y, 0, keepdims=False)
    col_own = lax.dynamic_index_in_dim(of_chip, c, 0, keepdims=False)
    col_there = lax.dynamic_index_in_dim(of_chip, 1 - c, 0, keepdims=False)
    halves = occupied.reshape(2, nj // 2, 1)
    pick = lambda half, col: (col[None, :] - halves[half]).reshape(1, -1)
    col_most = jnp.concatenate([pick(0, col_own), pick(0, col_there), pick(1, col_own)], axis=1)
    col_rest = pick(1, col_there)

    most = run(rows, row_e, col_most, [cols_early, early_there, cols_late])
    partial_term = run(rows, row_e, col_rest, [late_there], most)
    shares = lax.all_to_all(partial_term.reshape(nl * ny, slab, depth), ("l", "y"), 0, 0)
    density = jnp.sum(shares.astype(jnp.float32), axis=0)
    return density[:, None, :]


def solution(mesh):
    fine = Mesh(mesh.devices.reshape(12, 2, 2, 8, 2), ("z", "h", "l", "y", "c"))
    in_specs = (P(None, ("l", "y", "c"), ("z", "h")), P(), P())
    out_specs = P(("l", "y", "c"), ("z", "h"), None)
    return jax.shard_map(shards, mesh=fine, in_specs=in_specs, out_specs=out_specs, check_vma=False)
```

```python
import jax
import jax.numpy as jnp
from jax import lax
from jax.experimental import pallas as pl
from jax.experimental.pallas import tpu as pltpu
from jax.sharding import Mesh, PartitionSpec as P

occupied_base = -0.4
occupied_step = 0.01
virtual_base = 0.1
virtual_step = 0.01
spin_scale = 1.3

SWAP = [(0, 1), (1, 0)]


def load(cols_refs, full, sem):
    copies, first = [], 0
    for n, cols_ref in enumerate(cols_refs):
        chunks, width, lanes = cols_ref.shape
        for k in range(chunks):
            place = full.at[pl.ds(first, width), pl.ds(k * lanes, lanes)]
            copies.append(pltpu.make_async_copy(cols_ref.at[k], place, sem.at[n, k]))
        first += width
    for copy in copies:
        copy.start()
    for copy in copies:
        copy.wait()


def density_kernel(blocks, more, rows_ref, row_e, col_e, *refs):
    cols_refs, refs = refs[:blocks], refs[blocks:]
    before_ref = refs[0] if more else None
    out_ref, full, sem = refs[-3:]
    load(cols_refs, full, sem)
    pair = lax.dot_general(
        rows_ref[...], full[...], (((1,), (1,)), ((), ())), preferred_element_type=jnp.float32
    )
    amplitude = (spin_scale * pair / (row_e[...] + col_e[...])).astype(jnp.bfloat16)
    term = jnp.dot(amplitude, full[...], preferred_element_type=jnp.float32)
    if more:
        term = term + before_ref[...]
    out_ref[...] = term.astype(out_ref.dtype)


def run(rows, row_e, col_e, cols, before=None):
    blocks, more = len(cols), before is not None
    chunks = cols[0].shape[0]
    width = sum(block.shape[1] for block in cols)
    vmem = pl.BlockSpec(memory_space=pltpu.VMEM)
    anywhere = pl.BlockSpec(memory_space=pl.ANY)
    work = 4 * rows.size * width
    return pl.pallas_call(
        lambda *refs: density_kernel(blocks, more, *refs),
        out_shape=jax.ShapeDtypeStruct(rows.shape, jnp.bfloat16 if more else jnp.float32),
        in_specs=[vmem] * 3 + [anywhere] * blocks + [vmem] * more,
        out_specs=vmem,
        scratch_shapes=[
            pltpu.VMEM((width, rows.shape[1]), jnp.bfloat16),
            pltpu.SemaphoreType.DMA((blocks, chunks)),
        ],
        compiler_params=pltpu.CompilerParams(vmem_limit_bytes=24 * 1024 * 1024),
        cost_estimate=pl.CostEstimate(flops=work, bytes_accessed=work // 256, transcendentals=0),
    )(rows, row_e, jnp.concatenate(col_e, axis=1), *cols, *([before] if more else []))


def shards(integrals, occ_bins, vir_bins):
    nz, nh, nl, ny = (lax.axis_size(k) for k in ("z", "h", "l", "y"))
    z, h, l, y, c = (lax.axis_index(k) for k in ("z", "h", "l", "y", "c"))
    nj, slab, part = integrals.shape
    depth = nz * nh * part
    split = nj * slab // 3
    own = integrals.astype(jnp.bfloat16)
    packed = jnp.concatenate([own[: nj // 2], own[nj // 2 :]], axis=2)
    there = lax.ppermute(packed, "h", SWAP)
    other = jnp.concatenate([there[:, :, :part], there[:, :, part:]], axis=0)
    first = h == 0
    wide = jnp.concatenate([jnp.where(first, own, other), jnp.where(first, other, own)], axis=2)
    wide = wide.reshape(nj * slab, nh * part)
    seeds = lax.all_to_all(own, ("z", "h"), 0, 0)
    seeds = jnp.transpose(seeds, (1, 0, 2)).reshape(slab, depth)
    early, late = wide[:split], wide[split:]
    late = jnp.broadcast_to(late[None], (nz,) + late.shape)
    seeds, late = lax.optimization_barrier((seeds, late))
    cols_late = lax.all_to_all(late, "z", 0, 0)
    rows = lax.all_gather(seeds, "y", axis=0, tiled=True)
    early, rows = lax.optimization_barrier((early, rows))
    rows_there = lax.ppermute(rows, "l", SWAP)
    cols_early = lax.all_gather(early, "z", axis=0, tiled=False)
    cols_early, cols_late = lax.optimization_barrier((cols_early, cols_late))
    early_there = lax.ppermute(cols_early, "c", SWAP)
    late_there = lax.ppermute(cols_late, "c", SWAP)

    occupied = occupied_base - occupied_step * occ_bins.astype(jnp.float32)
    virtual = virtual_base + virtual_step * vir_bins.astype(jnp.float32)
    virtual = virtual.reshape(nl * ny, 2, slab)
    occ_own = lax.dynamic_index_in_dim(occupied, z * nh + h, 0, keepdims=False)
    row_e = (lax.dynamic_index_in_dim(virtual, c, 1, keepdims=False) - occ_own).reshape(-1, 1)
    of_chip = lax.dynamic_index_in_dim(virtual, l * ny + y, 0, keepdims=False)
    col_own = lax.dynamic_index_in_dim(of_chip, c, 0, keepdims=False)
    col_there = lax.dynamic_index_in_dim(of_chip, 1 - c, 0, keepdims=False)
    col_own = (col_own[None, :] - occupied[:, None]).reshape(1, -1)
    col_there = (col_there[None, :] - occupied[:, None]).reshape(1, -1)
    col_here = [col_own[:, split:], col_own[:, :split]]
    col_rest = [col_there[:, split:], col_there[:, :split]]

    both = jnp.concatenate([rows, rows_there], axis=0)
    rows = jnp.where(l == 0, both, jnp.concatenate([rows_there, rows], axis=0))
    here = run(rows, row_e, col_here, [cols_late, cols_early])
    partial_term = run(rows, row_e, col_rest, [late_there, early_there], here)
    shares = lax.all_to_all(partial_term.reshape(nl * ny, slab, depth), ("l", "y"), 0, 0)
    density = jnp.sum(shares.astype(jnp.float32), axis=0)
    return density[:, None, :]


def solution(mesh):
    fine = Mesh(mesh.devices.reshape(12, 2, 2, 8, 2), ("z", "h", "l", "y", "c"))
    in_specs = (P(None, ("l", "y", "c"), ("z", "h")), P(), P())
    out_specs = P(("l", "y", "c"), ("z", "h"), None)
    return jax.shard_map(shards, mesh=fine, in_specs=in_specs, out_specs=out_specs, check_vma=False)
```

```python
import jax
import jax.numpy as jnp
from jax import lax
from jax.experimental import pallas as pl
from jax.experimental.pallas import tpu as pltpu
from jax.sharding import Mesh, PartitionSpec as P

occupied_base = -0.4
occupied_step = 0.01
virtual_base = 0.1
virtual_step = 0.01
spin_scale = 1.3

SWAP = [(0, 1), (1, 0)]


def density_kernel(ahead, nz, more, rows_ref, row_e, col_e, *refs):
    cols_refs, refs = refs[: len(ahead)], refs[len(ahead) :]
    before_ref = refs[0] if more else None
    out_ref, full, sem = refs[-3:]
    z = lax.axis_index("z")
    copies = []
    for cols_ref, parts in zip(cols_refs, ahead):
        _, width, lanes = cols_ref.shape
        for k, (first, step) in enumerate(parts):
            place = pl.multiple_of(lax.rem(z + (step % nz), nz) * lanes, lanes)
            there = full.at[pl.ds(first, width), pl.ds(place, lanes)]
            copies.append(pltpu.make_async_copy(cols_ref.at[k], there, sem.at[len(copies)]))
    for copy in copies:
        copy.start()
    for copy in copies:
        copy.wait()
    pair = lax.dot_general(
        rows_ref[...], full[...], (((1,), (1,)), ((), ())), preferred_element_type=jnp.float32
    )
    amplitude = (spin_scale * pair / (row_e[...] + col_e[...])).astype(jnp.bfloat16)
    term = jnp.dot(amplitude, full[...], preferred_element_type=jnp.float32)
    if more:
        term = term + before_ref[...]
    out_ref[...] = term.astype(out_ref.dtype)


def run(nz, ahead, rows, row_e, col_e, cols, before=None):
    more, width = before is not None, col_e.shape[1]
    vmem = pl.BlockSpec(memory_space=pltpu.VMEM)
    anywhere = pl.BlockSpec(memory_space=pl.ANY)
    work = 4 * rows.size * width
    return pl.pallas_call(
        lambda *refs: density_kernel(ahead, nz, more, *refs),
        out_shape=jax.ShapeDtypeStruct(rows.shape, jnp.bfloat16 if more else jnp.float32),
        in_specs=[vmem] * 3 + [anywhere] * len(cols) + [vmem] * more,
        out_specs=vmem,
        scratch_shapes=[
            pltpu.VMEM((width, rows.shape[1]), jnp.bfloat16),
            pltpu.SemaphoreType.DMA((sum(len(parts) for parts in ahead),)),
        ],
        compiler_params=pltpu.CompilerParams(vmem_limit_bytes=24 * 1024 * 1024),
        cost_estimate=pl.CostEstimate(flops=work, bytes_accessed=work // 256, transcendentals=0),
    )(rows, row_e, col_e, *cols, *([before] if more else []))


def shards(integrals, occ_bins, vir_bins):
    nz, nh, nl, ny = (lax.axis_size(k) for k in ("z", "h", "l", "y"))
    z, h, l, y, c = (lax.axis_index(k) for k in ("z", "h", "l", "y", "c"))
    nj, slab, part = integrals.shape
    depth = nz * nh * part
    width = nj * slab
    own = integrals.astype(jnp.bfloat16)
    packed = jnp.concatenate([own[: nj // 2], own[nj // 2 :]], axis=2)
    there = lax.ppermute(packed, "h", SWAP)
    other = jnp.concatenate([there[:, :, :part], there[:, :, part:]], axis=0)
    first = h == 0
    wide = jnp.concatenate([jnp.where(first, own, other), jnp.where(first, other, own)], axis=2)
    wide = wide.reshape(width, nh * part)
    seeds = lax.all_to_all(own, ("z", "h"), 0, 0)
    seeds = jnp.transpose(seeds, (1, 0, 2)).reshape(slab, depth)
    seeds = jnp.broadcast_to(seeds[None], (nl * ny, slab, depth))

    def shift(block, by):
        return lax.ppermute(block, "z", [(k, (k + by) % nz) for k in range(nz)])

    up, down = shift(wide, 4), shift(wide, -4)
    up, down, seeds = lax.optimization_barrier((up, down, seeds))
    fours = jnp.stack([wide, up, down])
    below, above = shift(fours, 1), shift(fours, -1)
    last_above = shift(above[:, : width // 2], -1)
    last_below = shift(below[:, width // 2 :], 1)
    last = jnp.concatenate([last_above, last_below], axis=0)
    ones = jnp.concatenate([below, above], axis=0)
    here = [fours, below, above, last_above, last_below]
    tops = lambda *steps: [(0, step) for step in steps]
    ends = [(width // 2, step) for step in (-2, -6, 2)]
    of_here = [tops(0, -4, 4), tops(-1, -5, 3), tops(1, -3, 5), tops(2, -2, 6), ends]
    of_there = [of_here[0], of_here[1] + of_here[2], of_here[3] + ends]
    rows = lax.all_to_all(seeds, ("l", "y"), 0, 0).reshape(nl * ny * slab, depth)
    fours_there, ones_there, last_there = (lax.ppermute(k, "c", SWAP) for k in (fours, ones, last))

    occupied = occupied_base - occupied_step * occ_bins.astype(jnp.float32)
    virtual = virtual_base + virtual_step * vir_bins.astype(jnp.float32)
    virtual = virtual.reshape(nl * ny, 2, slab)
    occ_own = lax.dynamic_index_in_dim(occupied, z * nh + h, 0, keepdims=False)
    row_e = (lax.dynamic_index_in_dim(virtual, c, 1, keepdims=False) - occ_own).reshape(-1, 1)
    of_chip = lax.dynamic_index_in_dim(virtual, l * ny + y, 0, keepdims=False)
    col_own = lax.dynamic_index_in_dim(of_chip, c, 0, keepdims=False)
    col_there = lax.dynamic_index_in_dim(of_chip, 1 - c, 0, keepdims=False)
    col_own = (col_own[None, :] - occupied[:, None]).reshape(1, -1)
    col_there = (col_there[None, :] - occupied[:, None]).reshape(1, -1)

    before = run(nz, of_here, rows, row_e, col_own, here)
    there = [fours_there, ones_there, last_there]
    partial_term = run(nz, of_there, rows, row_e, col_there, there, before)
    shares = lax.all_to_all(partial_term.reshape(nl * ny, slab, depth), ("l", "y"), 0, 0)
    density = jnp.sum(shares.astype(jnp.float32), axis=0)
    return density[:, None, :]


def solution(mesh):
    fine = Mesh(mesh.devices.reshape(12, 2, 2, 8, 2), ("z", "h", "l", "y", "c"))
    in_specs = (P(None, ("l", "y", "c"), ("z", "h")), P(), P())
    out_specs = P(("l", "y", "c"), ("z", "h"), None)
    return jax.shard_map(shards, mesh=fine, in_specs=in_specs, out_specs=out_specs, check_vma=False)
```

```python
import jax
import jax.numpy as jnp
from jax import lax
from jax.experimental import pallas as pl
from jax.experimental.pallas import tpu as pltpu
from jax.sharding import Mesh, PartitionSpec as P

occupied_base = -0.4
occupied_step = 0.01
virtual_base = 0.1
virtual_step = 0.01
spin_scale = 1.3

SWAP = [(0, 1), (1, 0)]


def density_kernel(blocks, kinds, more, there_ref, there_e, own_ref, own_e, col_e, *refs):
    cols_refs, refs = refs[:blocks], refs[blocks:]
    befores, refs = (refs[:2], refs[2:]) if more else ((None, None), refs)
    outs, (full, sem) = refs[:2], refs[2:]
    copies, first, left = [], 0, 0
    for cols_ref in cols_refs:
        chunks, width, lanes = cols_ref.shape
        for k in range(chunks):
            there = full.at[pl.ds(first, width), pl.ds(left, lanes)]
            copies.append(pltpu.make_async_copy(cols_ref.at[k], there, sem.at[len(copies)]))
            left += lanes
        if left == full.shape[1]:
            first, left = first + width, 0
    for copy in copies:
        copy.start()
    for copy in copies:
        copy.wait()
    sides = ((there_ref, there_e, befores[0], outs[0]), (own_ref, own_e, befores[1], outs[1]))
    for rows_ref, row_e, before_ref, out_ref in sides:
        pair = lax.dot_general(
            rows_ref[...], full[...], (((1,), (1,)), ((), ())), preferred_element_type=jnp.float32
        )
        amplitude = (spin_scale * pair / (row_e[...] + col_e[...])).astype(jnp.bfloat16)
        term = jnp.dot(amplitude, full[...], preferred_element_type=jnp.float32)
        if more:
            term = term + before_ref[...]
        out_ref[...] = term.astype(out_ref.dtype)


def run(kinds, there, there_e, own, own_e, col_e, cols, befores=()):
    vmem = pl.BlockSpec(memory_space=pltpu.VMEM)
    anywhere = pl.BlockSpec(memory_space=pl.ANY)
    width = col_e.shape[1]
    work = 8 * own.size * width
    return pl.pallas_call(
        lambda *refs: density_kernel(len(cols), kinds, len(befores) > 0, *refs),
        out_shape=[jax.ShapeDtypeStruct(own.shape, kind) for kind in kinds],
        in_specs=[vmem] * 5 + [anywhere] * len(cols) + [vmem] * len(befores),
        out_specs=[vmem, vmem],
        scratch_shapes=[
            pltpu.VMEM((width, own.shape[1]), jnp.bfloat16),
            pltpu.SemaphoreType.DMA((sum(block.shape[0] for block in cols),)),
        ],
        compiler_params=pltpu.CompilerParams(vmem_limit_bytes=24 * 1024 * 1024),
        cost_estimate=pl.CostEstimate(flops=work, bytes_accessed=work // 256, transcendentals=0),
    )(there, there_e, own, own_e, col_e, *cols, *befores)


def shards(integrals, occ_bins, vir_bins):
    nz, nh, nl, ny = (lax.axis_size(k) for k in ("z", "h", "l", "y"))
    z, h, l, y, c = (lax.axis_index(k) for k in ("z", "h", "l", "y", "c"))
    nj, slab, part = integrals.shape
    depth = nz * nh * part
    own = integrals.astype(jnp.bfloat16).reshape(nz, nh, slab, part)
    even, odd = own[:, 0], own[:, 1]
    first = h == 0
    mine = jnp.where(first, even, odd)
    there = lax.ppermute(jnp.where(first, odd, even), "h", SWAP)
    wide = jnp.concatenate([jnp.where(first, mine, there), jnp.where(first, there, mine)], axis=2)
    seeds = lax.all_to_all(wide, "z", 0, 0)
    here = lax.all_gather(wide.reshape(nz * slab, nh * part), "z", axis=0, tiled=False)
    here, seeds = lax.optimization_barrier((here, seeds))

    def shift(block, by):
        ring = [(k, (k + by) % (nh * nl)) for k in range(nh * nl)]
        return lax.ppermute(block, ("h", "l"), ring)

    left, right = shift(here, 1), shift(here, -1)
    far_low, far_high = shift(left[: nz // 2], 1), shift(right[nz // 2 :], -1)
    seeds = jnp.transpose(seeds, (1, 0, 2)).reshape(slab, depth)
    rows = lax.all_to_all(jnp.broadcast_to(seeds[None], (ny, slab, depth)), "y", 0, 0)
    rows = rows.reshape(ny * slab, depth)
    rows_there = lax.ppermute(rows, "c", SWAP)

    occupied = occupied_base - occupied_step * occ_bins.astype(jnp.float32)
    virtual = virtual_base + virtual_step * vir_bins.astype(jnp.float32)
    virtual = virtual.reshape(nl, ny, 2, slab)
    occ_own = lax.dynamic_slice_in_dim(occupied, z * nh + h, 1, 0)
    core0, low0 = c == 0, l == 0
    of_rows = jnp.where(low0, virtual[0], virtual[1]) - occ_own
    own_e = jnp.where(core0, of_rows[:, 0], of_rows[:, 1]).reshape(-1, 1)
    there_e = jnp.where(core0, of_rows[:, 1], of_rows[:, 0]).reshape(-1, 1)
    of_cols = lax.dynamic_slice_in_dim(virtual, y, 1, 1)[:, 0]
    of_cols = jnp.where(core0, of_cols[:, 0], of_cols[:, 1])
    low_own = jnp.where(low0, of_cols[0], of_cols[1])
    low_other = jnp.where(low0, of_cols[1], of_cols[0])
    evens, odds = occupied[0::2], occupied[1::2]

    def col_e(low, is_even):
        return (low[None, :] - jnp.where(is_even, evens, odds)[:, None]).reshape(1, -1)

    most_e = [col_e(low_own, h == 0), col_e(low_other, h != l), col_e(low_other, h == l)]
    rest_e = col_e(low_own, h != 0)
    f32, bf16 = jnp.float32, jnp.bfloat16
    rows_e = (rows_there, there_e, rows, own_e)
    most = run((f32, f32), *rows_e, jnp.concatenate(most_e, axis=1), [here, left, right])
    for_there, for_own = run((bf16, f32), *rows_e, rest_e, [far_low, far_high], most)
    arrived = lax.ppermute(for_there, "c", SWAP)
    pair_sum = (for_own + arrived.astype(jnp.float32)).astype(jnp.bfloat16)
    shares = lax.all_to_all(pair_sum.reshape(ny, slab, depth), "y", 0, 0)
    density = jnp.sum(shares.astype(jnp.float32), axis=0)
    return density[:, None, :]


def solution(mesh):
    fine = Mesh(mesh.devices.reshape(12, 2, 2, 8, 2), ("z", "h", "l", "y", "c"))
    in_specs = (P(None, ("l", "y", "c"), ("z", "h")), P(), P())
    out_specs = P(("l", "y", "c"), ("z", "h"), None)
    return jax.shard_map(shards, mesh=fine, in_specs=in_specs, out_specs=out_specs, check_vma=False)
```

```python
import jax
import jax.numpy as jnp
from jax import lax
from jax.experimental import pallas as pl
from jax.experimental.pallas import tpu as pltpu
from jax.sharding import Mesh, PartitionSpec as P

occupied_base = -0.4
occupied_step = 0.01
virtual_base = 0.1
virtual_step = 0.01
spin_scale = 1.3

SWAP = [(0, 1), (1, 0)]


def density_kernel(halves, more, there_ref, there_e, own_ref, own_e, col_e, *refs):
    blocks, refs = refs[: len(halves)], refs[len(halves) :]
    befores, refs = (refs[:2], refs[2:]) if more else ((None, None), refs)
    outs, (full, sem) = refs[:2], refs[2:]
    h, l = lax.axis_index("h"), lax.axis_index("l")
    mixed = lax.rem(h + l, 2)
    parity = {"own": h, "far": 1 - h, "right": mixed, "left": 1 - mixed}
    copies = []
    for block, (side, first) in zip(blocks, halves):
        chunks, part, _ = block.shape
        for k in range(chunks):
            start = (first + k) * 2 * part + parity[side] * part
            place = full.at[pl.ds(pl.multiple_of(start, part), part)]
            copies.append(pltpu.make_async_copy(block.at[k], place, sem.at[len(copies)]))
    for copy in copies:
        copy.start()
    for copy in copies:
        copy.wait()
    sides = ((there_ref, there_e, befores[0], outs[0]), (own_ref, own_e, befores[1], outs[1]))
    for rows_ref, row_e, before_ref, out_ref in sides:
        pair = jnp.dot(rows_ref[...], full[...], preferred_element_type=jnp.float32)
        amplitude = (spin_scale * pair / (row_e[...] + col_e[...])).astype(jnp.bfloat16)
        term = lax.dot_general(
            amplitude, full[...], (((1,), (1,)), ((), ())), preferred_element_type=jnp.float32
        )
        if more:
            term = term + before_ref[...]
        out_ref[...] = term.astype(out_ref.dtype)


def run(kinds, there, there_e, own, own_e, col_e, halves, blocks, befores=()):
    vmem = pl.BlockSpec(memory_space=pltpu.VMEM)
    anywhere = pl.BlockSpec(memory_space=pl.ANY)
    width = col_e.shape[1]
    work = 8 * own.size * width
    return pl.pallas_call(
        lambda *refs: density_kernel(halves, len(befores) > 0, *refs),
        out_shape=[jax.ShapeDtypeStruct(own.shape, kind) for kind in kinds],
        in_specs=[vmem] * 5 + [anywhere] * len(blocks) + [vmem] * len(befores),
        out_specs=[vmem, vmem],
        scratch_shapes=[
            pltpu.VMEM((own.shape[1], width), jnp.bfloat16),
            pltpu.SemaphoreType.DMA((sum(block.shape[0] for block in blocks),)),
        ],
        compiler_params=pltpu.CompilerParams(vmem_limit_bytes=16 * 1024 * 1024),
        cost_estimate=pl.CostEstimate(flops=work, bytes_accessed=work // 256, transcendentals=0),
    )(there, there_e, own, own_e, col_e, *blocks, *befores)


def shards(integrals, occ_bins, vir_bins):
    nz, nh, nl, ny = (lax.axis_size(k) for k in ("z", "h", "l", "y"))
    z, h, l, y, c = (lax.axis_index(k) for k in ("z", "h", "l", "y", "c"))
    nj, slab, part = integrals.shape
    depth = nz * nh * part
    first, core0, low0 = h == 0, c == 0, l == 0
    rounded = integrals.astype(jnp.bfloat16)
    seeds = lax.all_to_all(rounded, ("z", "h"), 0, 0)
    own = jnp.transpose(rounded.reshape(nj * slab, part))
    here = lax.all_gather(own, "z", axis=0, tiled=False)
    here, seeds = lax.optimization_barrier((here, seeds))
    seeds = jnp.transpose(seeds, (1, 0, 2)).reshape(slab, depth)

    def shift(block, by):
        ring = [(k, (k + by) % (nh * nl)) for k in range(nh * nl)]
        return lax.ppermute(block, ("h", "l"), ring)

    mid = nz // 2
    low, high = here[:mid], here[mid:]
    left_low, right_high = shift(low, 1), shift(high, -1)
    left_high, right_low = shift(high, 1), shift(low, -1)
    far_low, far_high = shift(left_low, 1), shift(right_high, -1)
    rows = lax.all_to_all(jnp.broadcast_to(seeds[None], (ny, slab, depth)), "y", 0, 0)
    rows = rows.reshape(ny * slab, depth)
    rows_there = lax.ppermute(rows, "c", SWAP)

    occupied = occupied_base - occupied_step * occ_bins.astype(jnp.float32)
    virtual = virtual_base + virtual_step * vir_bins.astype(jnp.float32)
    virtual = virtual.reshape(nl, ny, 2, slab)
    occ_own = lax.dynamic_slice_in_dim(occupied, z * nh + h, 1, 0)
    of_rows = jnp.where(low0, virtual[0], virtual[1]) - occ_own
    own_e = jnp.where(core0, of_rows[:, 0], of_rows[:, 1]).reshape(-1, 1)
    there_e = jnp.where(core0, of_rows[:, 1], of_rows[:, 0]).reshape(-1, 1)
    of_cols = lax.dynamic_slice_in_dim(virtual, y, 1, 1)[:, 0]
    of_cols = jnp.where(core0, of_cols[:, 0], of_cols[:, 1])
    of_cols = (of_cols[:, None, :] - occupied[None, :, None]).reshape(nl, 1, nj * slab)
    col_own = jnp.where(low0, of_cols[0], of_cols[1])
    col_other = jnp.where(low0, of_cols[1], of_cols[0])

    f32, bf16 = jnp.float32, jnp.bfloat16
    rows_e = (rows_there, there_e, rows, own_e)
    sides = [("left", 0), ("right", mid), ("left", mid), ("right", 0)]
    blocks = [left_low, right_high, left_high, right_low]
    other = run((f32, f32), *rows_e, col_other, sides, blocks)
    sides = [("own", 0), ("far", 0), ("far", mid)]
    blocks = [here, far_low, far_high]
    for_there, for_own = run((bf16, f32), *rows_e, col_own, sides, blocks, other)
    arrived = lax.ppermute(for_there, "c", SWAP)
    pair_sum = (for_own + arrived.astype(jnp.float32)).astype(jnp.bfloat16)
    shares = lax.all_to_all(pair_sum.reshape(ny, slab, depth), "y", 0, 0)
    density = jnp.sum(shares.astype(jnp.float32), axis=0)
    return density[:, None, :]


def solution(mesh):
    fine = Mesh(mesh.devices.reshape(12, 2, 2, 8, 2), ("z", "h", "l", "y", "c"))
    in_specs = (P(None, ("l", "y", "c"), ("z", "h")), P(), P())
    out_specs = P(("l", "y", "c"), ("z", "h"), None)
    return jax.shard_map(shards, mesh=fine, in_specs=in_specs, out_specs=out_specs, check_vma=False)
```

```python
import jax
import jax.numpy as jnp
from jax import lax
from jax.experimental import pallas as pl
from jax.experimental.pallas import tpu as pltpu
from jax.sharding import Mesh, PartitionSpec as P

occupied_base = -0.4
occupied_step = 0.01
virtual_base = 0.1
virtual_step = 0.01
spin_scale = 1.3

SWAP = [(0, 1), (1, 0)]


def density_kernel(blocks, kinds, more, there_ref, there_e, own_ref, own_e, col_e, *refs):
    cols_refs, refs = refs[:blocks], refs[blocks:]
    befores, refs = (refs[:2], refs[2:]) if more else ((None, None), refs)
    outs, (full, sem) = refs[:2], refs[2:]
    copies, first, left = [], 0, 0
    for cols_ref in cols_refs:
        chunks, width, lanes = cols_ref.shape
        for k in range(chunks):
            there = full.at[pl.ds(first, width), pl.ds(left, lanes)]
            copies.append(pltpu.make_async_copy(cols_ref.at[k], there, sem.at[len(copies)]))
            left += lanes
        if left == full.shape[1]:
            first, left = first + width, 0
    for copy in copies:
        copy.start()
    for copy in copies:
        copy.wait()
    rows = jnp.concatenate([there_ref[...], own_ref[...]], axis=0)
    row_e = jnp.concatenate([there_e[...], own_e[...]], axis=0)
    pair = lax.dot_general(
        rows, full[...], (((1,), (1,)), ((), ())), preferred_element_type=jnp.float32
    )
    amplitude = (spin_scale * pair / (row_e + col_e[...])).astype(jnp.bfloat16)
    terms = jnp.dot(amplitude, full[...], preferred_element_type=jnp.float32)
    count = own_ref.shape[0]
    for term, before_ref, out_ref in zip((terms[:count], terms[count:]), befores, outs):
        if more:
            term = term + before_ref[...]
        out_ref[...] = term.astype(out_ref.dtype)


def run(kinds, there, there_e, own, own_e, col_e, cols, befores=()):
    vmem = pl.BlockSpec(memory_space=pltpu.VMEM)
    anywhere = pl.BlockSpec(memory_space=pl.ANY)
    width = col_e.shape[1]
    work = 8 * own.size * width
    return pl.pallas_call(
        lambda *refs: density_kernel(len(cols), kinds, len(befores) > 0, *refs),
        out_shape=[jax.ShapeDtypeStruct(own.shape, kind) for kind in kinds],
        in_specs=[vmem] * 5 + [anywhere] * len(cols) + [vmem] * len(befores),
        out_specs=[vmem, vmem],
        scratch_shapes=[
            pltpu.VMEM((width, own.shape[1]), jnp.bfloat16),
            pltpu.SemaphoreType.DMA((sum(block.shape[0] for block in cols),)),
        ],
        compiler_params=pltpu.CompilerParams(vmem_limit_bytes=14 * 1024 * 1024),
        cost_estimate=pl.CostEstimate(flops=work, bytes_accessed=work // 256, transcendentals=0),
    )(there, there_e, own, own_e, col_e, *cols, *befores)


def shards(integrals, occ_bins, vir_bins):
    nz, nh, nl, ny = (lax.axis_size(k) for k in ("z", "h", "l", "y"))
    z, h, l, y, c = (lax.axis_index(k) for k in ("z", "h", "l", "y", "c"))
    nj, slab, part = integrals.shape
    depth = nz * nh * part
    own = integrals.astype(jnp.bfloat16).reshape(nz, nh, slab, part)
    even, odd = own[:, 0], own[:, 1]
    first = h == 0
    mine = jnp.where(first, even, odd)
    there = lax.ppermute(jnp.where(first, odd, even), "h", SWAP)
    wide = jnp.concatenate([jnp.where(first, mine, there), jnp.where(first, there, mine)], axis=2)
    occupied = occupied_base - occupied_step * occ_bins.astype(jnp.float32)
    virtual = virtual_base + virtual_step * vir_bins.astype(jnp.float32)
    virtual = virtual.reshape(nl, ny, 2, slab)
    occ_own = lax.dynamic_slice_in_dim(occupied, z * nh + h, 1, 0)
    core0, low0 = c == 0, l == 0
    of_rows = jnp.where(low0, virtual[0], virtual[1]) - occ_own
    own_e = jnp.where(core0, of_rows[:, 0], of_rows[:, 1]).reshape(-1, 1)
    there_e = jnp.where(core0, of_rows[:, 1], of_rows[:, 0]).reshape(-1, 1)
    of_cols = lax.dynamic_slice_in_dim(virtual, y, 1, 1)[:, 0]
    of_cols = jnp.where(core0, of_cols[:, 0], of_cols[:, 1])
    low_own = jnp.where(low0, of_cols[0], of_cols[1])
    low_other = jnp.where(low0, of_cols[1], of_cols[0])
    evens, odds = occupied[0::2], occupied[1::2]

    def col_e(low, is_even):
        return (low[None, :] - jnp.where(is_even, evens, odds)[:, None]).reshape(1, -1)

    most_e = [col_e(low_own, h == 0), col_e(low_other, h != l), col_e(low_other, h == l)]
    rest_e = col_e(low_own, h != 0)
    wide, own_e, there_e, most_e, rest_e = lax.optimization_barrier(
        (wide, own_e, there_e, jnp.concatenate(most_e, axis=1), rest_e)
    )
    here = lax.all_gather(wide.reshape(nz * slab, nh * part), "z", axis=0, tiled=False)

    def shift(block, by):
        ring = [(k, (k + by) % (nh * nl)) for k in range(nh * nl)]
        return lax.ppermute(block, ("h", "l"), ring)

    left, right = shift(here, 1), shift(here, -1)
    far_low, far_high = shift(left[: nz // 2], 1), shift(right[nz // 2 :], -1)
    seeds = lax.dynamic_slice_in_dim(here, z * slab, slab, 1)
    seeds = jnp.transpose(seeds, (1, 0, 2)).reshape(slab, depth)
    rows = lax.all_to_all(jnp.broadcast_to(seeds[None], (ny, slab, depth)), "y", 0, 0)
    rows = rows.reshape(ny * slab, depth)
    rows_there = lax.ppermute(rows, "c", SWAP)

    f32, bf16 = jnp.float32, jnp.bfloat16
    rows_e = (rows_there, there_e, rows, own_e)
    most = run((f32, f32), *rows_e, most_e, [here, left, right])
    for_there, for_own = run((bf16, f32), *rows_e, rest_e, [far_low, far_high], most)
    arrived = lax.ppermute(for_there, "c", SWAP)
    pair_sum = (for_own + arrived.astype(jnp.float32)).astype(jnp.bfloat16)
    shares = lax.all_to_all(pair_sum.reshape(ny, slab, depth), "y", 0, 0)
    density = jnp.sum(shares.astype(jnp.float32), axis=0)
    return density[:, None, :]


def solution(mesh):
    fine = Mesh(mesh.devices.reshape(12, 2, 2, 8, 2), ("z", "h", "l", "y", "c"))
    in_specs = (P(None, ("l", "y", "c"), ("z", "h")), P(), P())
    out_specs = P(("l", "y", "c"), ("z", "h"), None)
    return jax.shard_map(shards, mesh=fine, in_specs=in_specs, out_specs=out_specs, check_vma=False)
```

```python
import jax
import jax.numpy as jnp
from jax import lax
from jax.experimental import pallas as pl
from jax.experimental.pallas import tpu as pltpu
from jax.sharding import Mesh, PartitionSpec as P

occupied_base = -0.4
occupied_step = 0.01
virtual_base = 0.1
virtual_step = 0.01
spin_scale = 1.3

SWAP = [(0, 1), (1, 0)]


def density_kernel(blocks, kinds, more, there_ref, there_e, own_ref, own_e, col_e, *refs):
    cols_refs, refs = refs[:blocks], refs[blocks:]
    befores, refs = (refs[:2], refs[2:]) if more else ((None, None), refs)
    outs, (full, sem) = refs[:2], refs[2:]
    copies, first, left = [], 0, 0
    for cols_ref in cols_refs:
        chunks, width, lanes = cols_ref.shape
        for k in range(chunks):
            there = full.at[pl.ds(first, width), pl.ds(left, lanes)]
            copies.append(pltpu.make_async_copy(cols_ref.at[k], there, sem.at[len(copies)]))
            left += lanes
        if left == full.shape[1]:
            first, left = first + width, 0
    for copy in copies:
        copy.start()
    for copy in copies:
        copy.wait()
    rows = jnp.concatenate([there_ref[...], own_ref[...]], axis=0)
    row_e = jnp.concatenate([there_e[...], own_e[...]], axis=0)
    pair = lax.dot_general(
        rows, full[...], (((1,), (1,)), ((), ())), preferred_element_type=jnp.float32
    )
    amplitude = (spin_scale * pair / (row_e + col_e[...])).astype(jnp.bfloat16)
    terms = jnp.dot(amplitude, full[...], preferred_element_type=jnp.float32)
    count = own_ref.shape[0]
    for term, before_ref, out_ref in zip((terms[:count], terms[count:]), befores, outs):
        if more:
            term = term + before_ref[...]
        out_ref[...] = term.astype(out_ref.dtype)


def run(kinds, there, there_e, own, own_e, col_e, cols, befores=()):
    vmem = pl.BlockSpec(memory_space=pltpu.VMEM)
    anywhere = pl.BlockSpec(memory_space=pl.ANY)
    width = col_e.shape[1]
    return pl.pallas_call(
        lambda *refs: density_kernel(len(cols), kinds, len(befores) > 0, *refs),
        out_shape=[jax.ShapeDtypeStruct(own.shape, kind) for kind in kinds],
        in_specs=[vmem] * 5 + [anywhere] * len(cols) + [vmem] * len(befores),
        out_specs=[vmem, vmem],
        scratch_shapes=[
            pltpu.VMEM((width, own.shape[1]), jnp.bfloat16),
            pltpu.SemaphoreType.DMA((sum(block.shape[0] for block in cols),)),
        ],
        compiler_params=pltpu.CompilerParams(vmem_limit_bytes=14 * 1024 * 1024),
        cost_estimate=pl.CostEstimate(flops=1024, bytes_accessed=1024, transcendentals=0),
    )(there, there_e, own, own_e, col_e, *cols, *befores)


def shards(integrals, occ_bins, vir_bins):
    nz, nh, nl, ny = (lax.axis_size(k) for k in ("z", "h", "l", "y"))
    z, h, l, y, c = (lax.axis_index(k) for k in ("z", "h", "l", "y", "c"))
    nj, slab, part = integrals.shape
    depth = nz * nh * part
    own = integrals.astype(jnp.bfloat16).reshape(nz, nh, slab, part)
    even, odd = own[:, 0], own[:, 1]
    first = h == 0
    mine = jnp.where(first, even, odd)
    there = lax.ppermute(jnp.where(first, odd, even), "h", SWAP)
    wide = jnp.concatenate([jnp.where(first, mine, there), jnp.where(first, there, mine)], axis=2)
    occupied = occupied_base - occupied_step * occ_bins.astype(jnp.float32)
    virtual = virtual_base + virtual_step * vir_bins.astype(jnp.float32)
    virtual = virtual.reshape(nl, ny, 2, slab)
    occ_own = lax.dynamic_slice_in_dim(occupied, z * nh + h, 1, 0)
    core0, low0 = c == 0, l == 0
    of_rows = jnp.where(low0, virtual[0], virtual[1]) - occ_own
    own_e = jnp.where(core0, of_rows[:, 0], of_rows[:, 1]).reshape(-1, 1)
    there_e = jnp.where(core0, of_rows[:, 1], of_rows[:, 0]).reshape(-1, 1)
    of_cols = lax.dynamic_slice_in_dim(virtual, y, 1, 1)[:, 0]
    of_cols = jnp.where(core0, of_cols[:, 0], of_cols[:, 1])
    low_own = jnp.where(low0, of_cols[0], of_cols[1])
    low_other = jnp.where(low0, of_cols[1], of_cols[0])
    evens, odds = occupied[0::2], occupied[1::2]

    def col_e(low, is_even):
        return (low[None, :] - jnp.where(is_even, evens, odds)[:, None]).reshape(1, -1)

    most_e = [col_e(low_own, h == 0), col_e(low_other, h != l), col_e(low_other, h == l)]
    rest_e = col_e(low_own, h != 0)
    wide, own_e, there_e, most_e, rest_e = lax.optimization_barrier(
        (wide, own_e, there_e, jnp.concatenate(most_e, axis=1), rest_e)
    )
    here = lax.all_gather(wide.reshape(nz * slab, nh * part), "z", axis=0, tiled=False)

    def shift(block, by):
        ring = [(k, (k + by) % (nh * nl)) for k in range(nh * nl)]
        return lax.ppermute(block, ("h", "l"), ring)

    left, right = shift(here, 1), shift(here, -1)
    far_low, far_high = shift(left[: nz // 2], 1), shift(right[nz // 2 :], -1)
    seeds = lax.dynamic_slice_in_dim(here, z * slab, slab, 1)
    seeds = jnp.transpose(seeds, (1, 0, 2)).reshape(slab, depth)
    rows = lax.all_to_all(jnp.broadcast_to(seeds[None], (ny, slab, depth)), "y", 0, 0)
    rows = rows.reshape(ny * slab, depth)
    rows_there = lax.ppermute(rows, "c", SWAP)

    f32, bf16 = jnp.float32, jnp.bfloat16
    rows_e = (rows_there, there_e, rows, own_e)
    most = run((f32, f32), *rows_e, most_e, [here, left, right])
    for_there, for_own = run((bf16, f32), *rows_e, rest_e, [far_low, far_high], most)
    arrived = lax.ppermute(for_there, "c", SWAP)
    pair_sum = (for_own + arrived.astype(jnp.float32)).astype(jnp.bfloat16)
    shares = lax.all_to_all(pair_sum.reshape(ny, slab, depth), "y", 0, 0)
    density = jnp.sum(shares.astype(jnp.float32), axis=0)
    return density[:, None, :]


def solution(mesh):
    fine = Mesh(mesh.devices.reshape(12, 2, 2, 8, 2), ("z", "h", "l", "y", "c"))
    in_specs = (P(None, ("l", "y", "c"), ("z", "h")), P(), P())
    out_specs = P(("l", "y", "c"), ("z", "h"), None)
    return jax.shard_map(shards, mesh=fine, in_specs=in_specs, out_specs=out_specs, check_vma=False)
```

```python
import jax
import jax.numpy as jnp
from jax import lax
from jax.experimental import pallas as pl
from jax.experimental.pallas import tpu as pltpu
from jax.sharding import Mesh, PartitionSpec as P

occupied_base = -0.4
occupied_step = 0.01
virtual_base = 0.1
virtual_step = 0.01
spin_scale = 1.3

SWAP = [(0, 1), (1, 0)]


def density_kernel(sides, blocks, more, col_e, *refs):
    rows_refs, refs = refs[:sides], refs[sides:]
    row_es, refs = refs[:sides], refs[sides:]
    cols_refs, refs = refs[:blocks], refs[blocks:]
    befores, refs = (refs[:sides], refs[sides:]) if more else ([None] * sides, refs)
    outs, (full, sem) = refs[:sides], refs[sides:]
    copies, first, left = [], 0, 0
    for cols_ref in cols_refs:
        chunks, width, lanes = cols_ref.shape
        for k in range(chunks):
            there = full.at[pl.ds(first, width), pl.ds(left, lanes)]
            copies.append(pltpu.make_async_copy(cols_ref.at[k], there, sem.at[len(copies)]))
            left += lanes
        if left == full.shape[1]:
            first, left = first + width, 0
    for copy in copies:
        copy.start()
    for copy in copies:
        copy.wait()
    rows = jnp.concatenate([ref[...] for ref in rows_refs], axis=0)
    row_e = jnp.concatenate([ref[...] for ref in row_es], axis=0)
    pair = lax.dot_general(
        rows, full[...], (((1,), (1,)), ((), ())), preferred_element_type=jnp.float32
    )
    amplitude = (spin_scale * pair / (row_e + col_e[...])).astype(jnp.bfloat16)
    terms = jnp.dot(amplitude, full[...], preferred_element_type=jnp.float32)
    count = outs[0].shape[0]
    for k, (before_ref, out_ref) in enumerate(zip(befores, outs)):
        term = terms[k * count : (k + 1) * count]
        if more:
            term = term + before_ref[...]
        out_ref[...] = term.astype(out_ref.dtype)


def run(kind, work, rows, row_es, col_e, cols, befores=()):
    vmem = pl.BlockSpec(memory_space=pltpu.VMEM)
    anywhere = pl.BlockSpec(memory_space=pl.ANY)
    sides, blocks = len(rows), len(cols)
    return pl.pallas_call(
        lambda *refs: density_kernel(sides, blocks, len(befores) > 0, *refs),
        out_shape=[jax.ShapeDtypeStruct(side.shape, kind) for side in rows],
        in_specs=[vmem] * (1 + 2 * sides) + [anywhere] * blocks + [vmem] * len(befores),
        out_specs=[vmem] * sides,
        scratch_shapes=[
            pltpu.VMEM((col_e.shape[1], rows[0].shape[1]), jnp.bfloat16),
            pltpu.SemaphoreType.DMA((sum(block.shape[0] for block in cols),)),
        ],
        compiler_params=pltpu.CompilerParams(vmem_limit_bytes=14 * 1024 * 1024),
        cost_estimate=pl.CostEstimate(flops=work, bytes_accessed=work // 256, transcendentals=0),
    )(col_e, *rows, *row_es, *cols, *befores)


def shards(integrals, occ_bins, vir_bins):
    nz, nh, nl, ny = (lax.axis_size(k) for k in ("z", "h", "l", "y"))
    z, h, l, y, c = (lax.axis_index(k) for k in ("z", "h", "l", "y", "c"))
    nj, slab, part = integrals.shape
    depth = nz * nh * part
    own = integrals.astype(jnp.bfloat16).reshape(nz, nh, slab, part)
    even, odd = own[:, 0], own[:, 1]
    first = h == 0
    mine = jnp.where(first, even, odd)
    there = lax.ppermute(jnp.where(first, odd, even), "h", SWAP)
    wide = jnp.concatenate([jnp.where(first, mine, there), jnp.where(first, there, mine)], axis=2)
    occupied = occupied_base - occupied_step * occ_bins.astype(jnp.float32)
    virtual = virtual_base + virtual_step * vir_bins.astype(jnp.float32)
    virtual = virtual.reshape(nl, ny, 2, slab)
    core0, low0 = c == 0, l == 0
    of_cols = lax.dynamic_slice_in_dim(virtual, y, 1, 1)[:, 0]
    of_cols = jnp.where(core0, of_cols[:, 0], of_cols[:, 1])
    low_own = jnp.where(low0, of_cols[0], of_cols[1])
    low_other = jnp.where(low0, of_cols[1], of_cols[0])
    evens, odds = occupied[0::2], occupied[1::2]

    def col_e(low, is_even):
        return (low[None, :] - jnp.where(is_even, evens, odds)[:, None]).reshape(1, -1)

    most_e = [col_e(low_own, h == 0), col_e(low_other, h != l), col_e(low_other, h == l)]
    rest_e = col_e(low_own, h != 0)
    wide, most_e, rest_e = lax.optimization_barrier((wide, jnp.concatenate(most_e, axis=1), rest_e))
    here = lax.all_gather(wide.reshape(nz * slab, nh * part), "z", axis=0, tiled=False)

    def shift(block, by):
        ring = [(k, (k + by) % (nh * nl)) for k in range(nh * nl)]
        return lax.ppermute(block, ("h", "l"), ring)

    left, right = shift(here, 1), shift(here, -1)
    far_low, far_high = shift(left[: nz // 2], 1), shift(right[nz // 2 :], -1)
    seeds = lax.dynamic_slice_in_dim(here, z * slab, slab, 1)
    seeds = jnp.transpose(seeds, (1, 0, 2)).reshape(slab, depth)
    rows = lax.all_to_all(jnp.broadcast_to(seeds[None], (ny, slab, depth)), "y", 0, 0)
    rows = rows.reshape(ny * slab, depth)
    rows, virtual, occupied = lax.optimization_barrier((rows, virtual, occupied))
    rows_there = lax.ppermute(rows, "c", SWAP)
    occ_own = lax.dynamic_slice_in_dim(occupied, z * nh + h, 1, 0)
    of_rows = jnp.where(low0, virtual[0], virtual[1]) - occ_own
    own_e = jnp.where(core0, of_rows[:, 0], of_rows[:, 1]).reshape(-1, 1)
    there_e = jnp.where(core0, of_rows[:, 1], of_rows[:, 0]).reshape(-1, 1)

    f32, bf16 = jnp.float32, jnp.bfloat16
    both, both_e = [rows_there, rows], [there_e, own_e]
    far, work = [far_low, far_high], 4 * rest_e.size * rows.size
    most = run(f32, 1024, both, both_e, most_e, [here, left, right])
    (for_there,) = run(bf16, work, both[:1], both_e[:1], rest_e, far, most[:1])
    arrived = lax.ppermute(for_there, "c", SWAP)
    (for_own,) = run(f32, work, both[1:], both_e[1:], rest_e, far, most[1:])
    pair_sum = (for_own + arrived.astype(jnp.float32)).astype(jnp.bfloat16)
    shares = lax.all_to_all(pair_sum.reshape(ny, slab, depth), "y", 0, 0)
    density = jnp.sum(shares.astype(jnp.float32), axis=0)
    return density[:, None, :]


def solution(mesh):
    fine = Mesh(mesh.devices.reshape(12, 2, 2, 8, 2), ("z", "h", "l", "y", "c"))
    in_specs = (P(None, ("l", "y", "c"), ("z", "h")), P(), P())
    out_specs = P(("l", "y", "c"), ("z", "h"), None)
    return jax.shard_map(shards, mesh=fine, in_specs=in_specs, out_specs=out_specs, check_vma=False)
```

```python
import jax
import jax.numpy as jnp
from jax import lax
from jax.experimental import pallas as pl
from jax.experimental.pallas import tpu as pltpu
from jax.sharding import Mesh, PartitionSpec as P

occupied_base = -0.4
occupied_step = 0.01
virtual_base = 0.1
virtual_step = 0.01
spin_scale = 1.3

SWAP = [(0, 1), (1, 0)]


def density_kernel(sides, blocks, more, col_e, *refs):
    rows_refs, refs = refs[:sides], refs[sides:]
    row_es, refs = refs[:sides], refs[sides:]
    cols_refs, refs = refs[:blocks], refs[blocks:]
    befores, refs = (refs[:sides], refs[sides:]) if more else ([None] * sides, refs)
    outs, (full, sem) = refs[:sides], refs[sides:]
    copies, first, left = [], 0, 0
    for cols_ref in cols_refs:
        chunks, width, lanes = cols_ref.shape
        for k in range(chunks):
            there = full.at[pl.ds(first, width), pl.ds(left, lanes)]
            copies.append(pltpu.make_async_copy(cols_ref.at[k], there, sem.at[len(copies)]))
            left += lanes
        if left == full.shape[1]:
            first, left = first + width, 0
    for copy in copies:
        copy.start()
    for copy in copies:
        copy.wait()
    rows = jnp.concatenate([ref[...] for ref in rows_refs], axis=0)
    row_e = jnp.concatenate([ref[...] for ref in row_es], axis=0)
    pair = lax.dot_general(
        rows, full[...], (((1,), (1,)), ((), ())), preferred_element_type=jnp.float32
    )
    amplitude = (spin_scale * pair / (row_e + col_e[...])).astype(jnp.bfloat16)
    terms = jnp.dot(amplitude, full[...], preferred_element_type=jnp.float32)
    count = outs[0].shape[0]
    for k, (before_ref, out_ref) in enumerate(zip(befores, outs)):
        term = terms[k * count : (k + 1) * count]
        if more:
            term = term + before_ref[...]
        out_ref[...] = term.astype(out_ref.dtype)


def run(kinds, work, rows, row_es, col_e, cols, befores=()):
    vmem = pl.BlockSpec(memory_space=pltpu.VMEM)
    anywhere = pl.BlockSpec(memory_space=pl.ANY)
    sides, blocks = len(rows), len(cols)
    return pl.pallas_call(
        lambda *refs: density_kernel(sides, blocks, len(befores) > 0, *refs),
        out_shape=[jax.ShapeDtypeStruct(side.shape, kind) for side, kind in zip(rows, kinds)],
        in_specs=[vmem] * (1 + 2 * sides) + [anywhere] * blocks + [vmem] * len(befores),
        out_specs=[vmem] * sides,
        scratch_shapes=[
            pltpu.VMEM((col_e.shape[1], rows[0].shape[1]), jnp.bfloat16),
            pltpu.SemaphoreType.DMA((sum(block.shape[0] for block in cols),)),
        ],
        compiler_params=pltpu.CompilerParams(vmem_limit_bytes=14 * 1024 * 1024),
        cost_estimate=pl.CostEstimate(flops=work, bytes_accessed=work // 256, transcendentals=0),
    )(col_e, *rows, *row_es, *cols, *befores)


def shards(integrals, occ_bins, vir_bins):
    nz, nh, nl, ny = (lax.axis_size(k) for k in ("z", "h", "l", "y"))
    z, h, l, y, c = (lax.axis_index(k) for k in ("z", "h", "l", "y", "c"))
    nj, slab, part = integrals.shape
    depth = nz * nh * part
    own = integrals.astype(jnp.bfloat16).reshape(nz, nh, slab, part)
    even, odd = own[:, 0], own[:, 1]
    first = h == 0
    mine = jnp.where(first, even, odd)
    there = lax.ppermute(jnp.where(first, odd, even), "h", SWAP)
    wide = jnp.concatenate([jnp.where(first, mine, there), jnp.where(first, there, mine)], axis=2)
    occupied = occupied_base - occupied_step * occ_bins.astype(jnp.float32)
    virtual = virtual_base + virtual_step * vir_bins.astype(jnp.float32)
    virtual = virtual.reshape(nl, ny, 2, slab)
    core0, low0 = c == 0, l == 0
    of_cols = lax.dynamic_slice_in_dim(virtual, y, 1, 1)[:, 0]
    of_cols = jnp.where(core0, of_cols[:, 0], of_cols[:, 1])
    low_own = jnp.where(low0, of_cols[0], of_cols[1])
    low_other = jnp.where(low0, of_cols[1], of_cols[0])
    evens, odds = occupied[0::2], occupied[1::2]

    def col_e(low, is_even):
        return (low[None, :] - jnp.where(is_even, evens, odds)[:, None]).reshape(1, -1)

    near_even = (h != l) == core0
    most_e = [col_e(low_own, h == 0), col_e(low_other, near_even), col_e(low_other, ~near_even)]
    rest_e = col_e(low_own, h != 0)
    wide, most_e, rest_e = lax.optimization_barrier((wide, jnp.concatenate(most_e, axis=1), rest_e))
    here = lax.all_gather(wide.reshape(nz * slab, nh * part), "z", axis=0, tiled=False)

    def shift(block, by):
        count = nh * nl
        ring = [(2 * k, 2 * ((k + by) % count)) for k in range(count)]
        ring += [(2 * k + 1, 2 * ((k - by) % count) + 1) for k in range(count)]
        return lax.ppermute(block, ("h", "l", "c"), ring)

    near, off = shift(here, 1), shift(here, -1)
    far = shift(near, 1)
    seeds = lax.dynamic_slice_in_dim(here, z * slab, slab, 1)
    seeds = jnp.transpose(seeds, (1, 0, 2)).reshape(slab, depth)
    rows = lax.all_to_all(jnp.broadcast_to(seeds[None], (ny, slab, depth)), "y", 0, 0)
    rows = rows.reshape(ny * slab, depth)
    rows, virtual, occupied = lax.optimization_barrier((rows, virtual, occupied))
    rows_there = lax.ppermute(rows, "c", SWAP)
    occ_own = lax.dynamic_slice_in_dim(occupied, z * nh + h, 1, 0)
    of_rows = jnp.where(low0, virtual[0], virtual[1]) - occ_own
    own_e = jnp.where(core0, of_rows[:, 0], of_rows[:, 1]).reshape(-1, 1)
    there_e = jnp.where(core0, of_rows[:, 1], of_rows[:, 0]).reshape(-1, 1)

    f32, bf16 = jnp.float32, jnp.bfloat16
    both, both_e = [rows_there, rows], [there_e, own_e]
    work = 8 * rest_e.size * rows.size
    most = run((f32, f32), 1024, both, both_e, most_e, [here, near, off])
    for_there, for_own = run((bf16, f32), work, both, both_e, rest_e, [far], most)
    arrived = lax.ppermute(for_there, "c", SWAP)
    pair_sum = (for_own + arrived.astype(jnp.float32)).astype(jnp.bfloat16)
    shares = lax.all_to_all(pair_sum.reshape(ny, slab, depth), "y", 0, 0)
    density = jnp.sum(shares.astype(jnp.float32), axis=0)
    return density[:, None, :]


def solution(mesh):
    fine = Mesh(mesh.devices.reshape(12, 2, 2, 8, 2), ("z", "h", "l", "y", "c"))
    in_specs = (P(None, ("l", "y", "c"), ("z", "h")), P(), P())
    out_specs = P(("l", "y", "c"), ("z", "h"), None)
    return jax.shard_map(shards, mesh=fine, in_specs=in_specs, out_specs=out_specs, check_vma=False)
```

```python
import jax
import jax.numpy as jnp
from jax import lax
from jax.experimental import pallas as pl
from jax.experimental.pallas import tpu as pltpu
from jax.sharding import Mesh, PartitionSpec as P

occupied_base = -0.4
occupied_step = 0.01
virtual_base = 0.1
virtual_step = 0.01
spin_scale = 1.3

SWAP = [(0, 1), (1, 0)]


def density_kernel(sides, blocks, more, col_e, *refs):
    rows_refs, refs = refs[:sides], refs[sides:]
    row_es, refs = refs[:sides], refs[sides:]
    cols_refs, refs = refs[:blocks], refs[blocks:]
    befores, refs = (refs[:sides], refs[sides:]) if more else ([None] * sides, refs)
    outs, (full, sem) = refs[:sides], refs[sides:]
    copies, first, left = [], 0, 0
    for cols_ref in cols_refs:
        chunks, width, lanes = cols_ref.shape
        for k in range(chunks):
            there = full.at[pl.ds(first, width), pl.ds(left, lanes)]
            copies.append(pltpu.make_async_copy(cols_ref.at[k], there, sem.at[len(copies)]))
            left += lanes
        if left == full.shape[1]:
            first, left = first + width, 0
    for copy in copies:
        copy.start()
    for copy in copies:
        copy.wait()
    rows = jnp.concatenate([ref[...] for ref in rows_refs], axis=0)
    row_e = jnp.concatenate([ref[...] for ref in row_es], axis=0)
    pair = lax.dot_general(
        rows, full[...], (((1,), (1,)), ((), ())), preferred_element_type=jnp.float32
    )
    amplitude = (spin_scale * pair / (row_e + col_e[...])).astype(jnp.bfloat16)
    terms = jnp.dot(amplitude, full[...], preferred_element_type=jnp.float32)
    count = outs[0].shape[0]
    for k, (before_ref, out_ref) in enumerate(zip(befores, outs)):
        term = terms[k * count : (k + 1) * count]
        if more:
            term = term + before_ref[...]
        out_ref[...] = term.astype(out_ref.dtype)


def run(kinds, work, rows, row_es, col_e, cols, befores=()):
    vmem = pl.BlockSpec(memory_space=pltpu.VMEM)
    anywhere = pl.BlockSpec(memory_space=pl.ANY)
    sides, blocks = len(rows), len(cols)
    return pl.pallas_call(
        lambda *refs: density_kernel(sides, blocks, len(befores) > 0, *refs),
        out_shape=[jax.ShapeDtypeStruct(side.shape, kind) for side, kind in zip(rows, kinds)],
        in_specs=[vmem] * (1 + 2 * sides) + [anywhere] * blocks + [vmem] * len(befores),
        out_specs=[vmem] * sides,
        scratch_shapes=[
            pltpu.VMEM((col_e.shape[1], rows[0].shape[1]), jnp.bfloat16),
            pltpu.SemaphoreType.DMA((sum(block.shape[0] for block in cols),)),
        ],
        compiler_params=pltpu.CompilerParams(vmem_limit_bytes=14 * 1024 * 1024),
        cost_estimate=pl.CostEstimate(flops=work, bytes_accessed=work // 256, transcendentals=0),
    )(col_e, *rows, *row_es, *cols, *befores)


def shards(integrals, occ_bins, vir_bins):
    nz, nh, nl, ny = (lax.axis_size(k) for k in ("z", "h", "l", "y"))
    z, h, l, y, c = (lax.axis_index(k) for k in ("z", "h", "l", "y", "c"))
    nj, slab, part = integrals.shape
    depth = nz * nh * part
    own = integrals.astype(jnp.bfloat16).reshape(nz, nh, slab, part)
    even, odd = own[:, 0], own[:, 1]
    first = h == 0
    mine = jnp.where(first, even, odd)
    there = lax.ppermute(jnp.where(first, odd, even), "h", SWAP)
    wide = jnp.concatenate([jnp.where(first, mine, there), jnp.where(first, there, mine)], axis=2)
    occupied = occupied_base - occupied_step * occ_bins.astype(jnp.float32)
    virtual = virtual_base + virtual_step * vir_bins.astype(jnp.float32)
    virtual = virtual.reshape(nl, ny, 2, slab)
    core0, low0 = c == 0, l == 0
    of_cols = lax.dynamic_slice_in_dim(virtual, y, 1, 1)[:, 0]
    of_cols = jnp.where(core0, of_cols[:, 0], of_cols[:, 1])
    low_own = jnp.where(low0, of_cols[0], of_cols[1])
    low_other = jnp.where(low0, of_cols[1], of_cols[0])
    evens, odds = occupied[0::2], occupied[1::2]

    def col_e(low, is_even):
        return (low[None, :] - jnp.where(is_even, evens, odds)[:, None]).reshape(1, -1)

    near_even = (h != l) == core0
    most_e = [col_e(low_own, h == 0), col_e(low_other, near_even)]
    rest_e = [col_e(low_other, ~near_even), col_e(low_own, h != 0)]
    most_e, rest_e = jnp.concatenate(most_e, axis=1), jnp.concatenate(rest_e, axis=1)
    wide, most_e, rest_e = lax.optimization_barrier((wide, most_e, rest_e))
    here = lax.all_gather(wide.reshape(nz * slab, nh * part), "z", axis=0, tiled=False)

    def shift(block, by):
        count = nh * nl
        ring = [(2 * k, 2 * ((k + by) % count)) for k in range(count)]
        ring += [(2 * k + 1, 2 * ((k - by) % count) + 1) for k in range(count)]
        return lax.ppermute(block, ("h", "l", "c"), ring)

    near, off = shift(here, 1), shift(here, -1)
    far = shift(near, 1)
    seeds = lax.dynamic_slice_in_dim(here, z * slab, slab, 1)
    seeds = jnp.transpose(seeds, (1, 0, 2)).reshape(slab, depth)
    rows = lax.all_to_all(jnp.broadcast_to(seeds[None], (ny, slab, depth)), "y", 0, 0)
    rows = rows.reshape(ny * slab, depth)
    rows, virtual, occupied = lax.optimization_barrier((rows, virtual, occupied))
    rows_there = lax.ppermute(rows, "c", SWAP)
    occ_own = lax.dynamic_slice_in_dim(occupied, z * nh + h, 1, 0)
    of_rows = jnp.where(low0, virtual[0], virtual[1]) - occ_own
    own_e = jnp.where(core0, of_rows[:, 0], of_rows[:, 1]).reshape(-1, 1)
    there_e = jnp.where(core0, of_rows[:, 1], of_rows[:, 0]).reshape(-1, 1)

    f32, bf16 = jnp.float32, jnp.bfloat16
    both, both_e = [rows_there, rows], [there_e, own_e]
    work = 8 * rest_e.size * rows.size
    most = run((f32, f32), 1024, both, both_e, most_e, [here, near])
    for_there, for_own = run((bf16, f32), work, both, both_e, rest_e, [off, far], most)
    arrived = lax.ppermute(for_there, "c", SWAP)
    pair_sum = (for_own + arrived.astype(jnp.float32)).astype(jnp.bfloat16)
    shares = lax.all_to_all(pair_sum.reshape(ny, slab, depth), "y", 0, 0)
    density = jnp.sum(shares.astype(jnp.float32), axis=0)
    return density[:, None, :]


def solution(mesh):
    fine = Mesh(mesh.devices.reshape(12, 2, 2, 8, 2), ("z", "h", "l", "y", "c"))
    in_specs = (P(None, ("l", "y", "c"), ("z", "h")), P(), P())
    out_specs = P(("l", "y", "c"), ("z", "h"), None)
    return jax.shard_map(shards, mesh=fine, in_specs=in_specs, out_specs=out_specs, check_vma=False)
```

```python
import jax
import jax.numpy as jnp
from jax import lax
from jax.experimental import pallas as pl
from jax.experimental.pallas import tpu as pltpu
from jax.sharding import Mesh, PartitionSpec as P

occupied_base = -0.4
occupied_step = 0.01
virtual_base = 0.1
virtual_step = 0.01
spin_scale = 1.3

SWAP = [(0, 1), (1, 0)]


def density_kernel(sides, blocks, more, col_e, *refs):
    rows_refs, refs = refs[:sides], refs[sides:]
    row_es, refs = refs[:sides], refs[sides:]
    cols_refs, refs = refs[:blocks], refs[blocks:]
    befores, refs = (refs[:sides], refs[sides:]) if more else ([None] * sides, refs)
    outs, (full, sem) = refs[:sides], refs[sides:]
    copies, first, left = [], 0, 0
    for cols_ref in cols_refs:
        chunks, width, lanes = cols_ref.shape
        for k in range(chunks):
            there = full.at[pl.ds(first, width), pl.ds(left, lanes)]
            copies.append(pltpu.make_async_copy(cols_ref.at[k], there, sem.at[len(copies)]))
            left += lanes
        if left == full.shape[1]:
            first, left = first + width, 0
    for copy in copies:
        copy.start()
    for copy in copies:
        copy.wait()
    rows = jnp.concatenate([ref[...] for ref in rows_refs], axis=0)
    row_e = jnp.concatenate([ref[...] for ref in row_es], axis=0)
    pair = lax.dot_general(
        rows, full[...], (((1,), (1,)), ((), ())), preferred_element_type=jnp.float32
    )
    amplitude = (spin_scale * pair / (row_e + col_e[...])).astype(jnp.bfloat16)
    terms = jnp.dot(amplitude, full[...], preferred_element_type=jnp.float32)
    count = outs[0].shape[0]
    for k, (before_ref, out_ref) in enumerate(zip(befores, outs)):
        term = terms[k * count : (k + 1) * count]
        if more:
            term = term + before_ref[...]
        out_ref[...] = term.astype(out_ref.dtype)


def run(kinds, work, rows, row_es, col_e, cols, befores=()):
    vmem = pl.BlockSpec(memory_space=pltpu.VMEM)
    anywhere = pl.BlockSpec(memory_space=pl.ANY)
    sides, blocks = len(rows), len(cols)
    return pl.pallas_call(
        lambda *refs: density_kernel(sides, blocks, len(befores) > 0, *refs),
        out_shape=[jax.ShapeDtypeStruct(side.shape, kind) for side, kind in zip(rows, kinds)],
        in_specs=[vmem] * (1 + 2 * sides) + [anywhere] * blocks + [vmem] * len(befores),
        out_specs=[vmem] * sides,
        scratch_shapes=[
            pltpu.VMEM((col_e.shape[1], rows[0].shape[1]), jnp.bfloat16),
            pltpu.SemaphoreType.DMA((sum(block.shape[0] for block in cols),)),
        ],
        compiler_params=pltpu.CompilerParams(vmem_limit_bytes=14 * 1024 * 1024),
        cost_estimate=pl.CostEstimate(flops=work, bytes_accessed=work // 256, transcendentals=0),
    )(col_e, *rows, *row_es, *cols, *befores)


def shards(integrals, occ_bins, vir_bins):
    nz, nh, nl, ny = (lax.axis_size(k) for k in ("z", "h", "l", "y"))
    z, h, l, y, c = (lax.axis_index(k) for k in ("z", "h", "l", "y", "c"))
    nj, slab, part = integrals.shape
    depth = nz * nh * part
    own = integrals.astype(jnp.bfloat16).reshape(nz, nh, slab, part)
    even, odd = own[:, 0], own[:, 1]
    first = h == 0
    mine = jnp.where(first, even, odd)
    there = lax.ppermute(jnp.where(first, odd, even), "h", SWAP)
    wide = jnp.concatenate([jnp.where(first, mine, there), jnp.where(first, there, mine)], axis=2)
    occupied = occupied_base - occupied_step * occ_bins.astype(jnp.float32)
    virtual = virtual_base + virtual_step * vir_bins.astype(jnp.float32)
    virtual = virtual.reshape(nl, ny, 2, slab)
    core0, low0 = c == 0, l == 0
    of_cols = lax.dynamic_slice_in_dim(virtual, y, 1, 1)[:, 0]
    of_cols = jnp.where(core0, of_cols[:, 0], of_cols[:, 1])
    low_own = jnp.where(low0, of_cols[0], of_cols[1])
    low_other = jnp.where(low0, of_cols[1], of_cols[0])
    evens, odds = occupied[0::2], occupied[1::2]

    def col_e(low, is_even):
        return (low[None, :] - jnp.where(is_even, evens, odds)[:, None]).reshape(1, -1)

    near_even = (h != l) == core0
    most_e = [col_e(low_own, h == 0), col_e(low_other, near_even), col_e(low_other, ~near_even)]
    rest_e = col_e(low_own, h != 0)
    wide, most_e, rest_e = lax.optimization_barrier((wide, jnp.concatenate(most_e, axis=1), rest_e))
    here = lax.all_gather(wide.reshape(nz * slab, nh * part), "z", axis=0, tiled=False)

    def shift(block, by):
        count = nh * nl
        ring = [(2 * k, 2 * ((k + by) % count)) for k in range(count)]
        ring += [(2 * k + 1, 2 * ((k - by) % count) + 1) for k in range(count)]
        return lax.ppermute(block, ("h", "l", "c"), ring)

    near, off = shift(here, 1), shift(here, -1)
    near, off = lax.optimization_barrier((near, off))
    far = shift(near, 1)
    seeds = lax.dynamic_slice_in_dim(here, z * slab, slab, 1)
    seeds = jnp.transpose(seeds, (1, 0, 2)).reshape(slab, depth)
    rows = lax.all_to_all(jnp.broadcast_to(seeds[None], (ny, slab, depth)), "y", 0, 0)
    rows = rows.reshape(ny * slab, depth)
    rows, virtual, occupied = lax.optimization_barrier((rows, virtual, occupied))
    rows_there = lax.ppermute(rows, "c", SWAP)
    occ_own = lax.dynamic_slice_in_dim(occupied, z * nh + h, 1, 0)
    of_rows = jnp.where(low0, virtual[0], virtual[1]) - occ_own
    own_e = jnp.where(core0, of_rows[:, 0], of_rows[:, 1]).reshape(-1, 1)
    there_e = jnp.where(core0, of_rows[:, 1], of_rows[:, 0]).reshape(-1, 1)

    f32, bf16 = jnp.float32, jnp.bfloat16
    both, both_e = [rows_there, rows], [there_e, own_e]
    work = 8 * rest_e.size * rows.size
    most = run((f32, f32), 1024, both, both_e, most_e, [here, near, off])
    for_there, for_own = run((bf16, f32), work, both, both_e, rest_e, [far], most)
    arrived = lax.ppermute(for_there, "c", SWAP)
    pair_sum = (for_own + arrived.astype(jnp.float32)).astype(jnp.bfloat16)
    shares = lax.all_to_all(pair_sum.reshape(ny, slab, depth), "y", 0, 0)
    density = jnp.sum(shares.astype(jnp.float32), axis=0)
    return density[:, None, :]


def solution(mesh):
    fine = Mesh(mesh.devices.reshape(12, 2, 2, 8, 2), ("z", "h", "l", "y", "c"))
    in_specs = (P(None, ("l", "y", "c"), ("z", "h")), P(), P())
    out_specs = P(("l", "y", "c"), ("z", "h"), None)
    return jax.shard_map(shards, mesh=fine, in_specs=in_specs, out_specs=out_specs, check_vma=False)
```

```python
import jax
import jax.numpy as jnp
from jax import lax
from jax.experimental import pallas as pl
from jax.experimental.pallas import tpu as pltpu
from jax.sharding import Mesh, PartitionSpec as P

occupied_base = -0.4
occupied_step = 0.01
virtual_base = 0.1
virtual_step = 0.01
spin_scale = 1.3

SWAP = [(0, 1), (1, 0)]


def density_kernel(sides, blocks, more, col_e, *refs):
    rows_refs, refs = refs[:sides], refs[sides:]
    row_es, refs = refs[:sides], refs[sides:]
    cols_refs, refs = refs[:blocks], refs[blocks:]
    befores, refs = (refs[:sides], refs[sides:]) if more else ([None] * sides, refs)
    outs, (full, sem) = refs[:sides], refs[sides:]
    copies, first, left = [], 0, 0
    for cols_ref in cols_refs:
        chunks, width, lanes = cols_ref.shape
        for k in range(chunks):
            there = full.at[pl.ds(first, width), pl.ds(left, lanes)]
            copies.append(pltpu.make_async_copy(cols_ref.at[k], there, sem.at[len(copies)]))
            left += lanes
        if left == full.shape[1]:
            first, left = first + width, 0
    for copy in copies:
        copy.start()
    rows = jnp.concatenate([ref[...] for ref in rows_refs], axis=0)
    row_e = jnp.concatenate([ref[...] for ref in row_es], axis=0)
    lanes = cols_refs[0].shape[2]
    middle = full.shape[1] // lanes // 2 * lanes
    starts = [k % (full.shape[1] // lanes) * lanes for k in range(len(copies))]
    pair = None
    for low, high in ((0, middle), (middle, full.shape[1])):
        for copy, start in zip(copies, starts):
            if low <= start < high:
                copy.wait()
        part = lax.dot_general(
            rows[:, low:high],
            full[:, low:high],
            (((1,), (1,)), ((), ())),
            preferred_element_type=jnp.float32,
        )
        pair = part if pair is None else pair + part
    amplitude = (spin_scale * pair / (row_e + col_e[...])).astype(jnp.bfloat16)
    terms = jnp.dot(amplitude, full[...], preferred_element_type=jnp.float32)
    count = outs[0].shape[0]
    for k, (before_ref, out_ref) in enumerate(zip(befores, outs)):
        term = terms[k * count : (k + 1) * count]
        if more:
            term = term + before_ref[...]
        out_ref[...] = term.astype(out_ref.dtype)


def run(kinds, work, rows, row_es, col_e, cols, befores=()):
    vmem = pl.BlockSpec(memory_space=pltpu.VMEM)
    anywhere = pl.BlockSpec(memory_space=pl.ANY)
    sides, blocks = len(rows), len(cols)
    return pl.pallas_call(
        lambda *refs: density_kernel(sides, blocks, len(befores) > 0, *refs),
        out_shape=[jax.ShapeDtypeStruct(side.shape, kind) for side, kind in zip(rows, kinds)],
        in_specs=[vmem] * (1 + 2 * sides) + [anywhere] * blocks + [vmem] * len(befores),
        out_specs=[vmem] * sides,
        scratch_shapes=[
            pltpu.VMEM((col_e.shape[1], rows[0].shape[1]), jnp.bfloat16),
            pltpu.SemaphoreType.DMA((sum(block.shape[0] for block in cols),)),
        ],
        compiler_params=pltpu.CompilerParams(vmem_limit_bytes=14 * 1024 * 1024),
        cost_estimate=pl.CostEstimate(flops=work, bytes_accessed=work // 256, transcendentals=0),
    )(col_e, *rows, *row_es, *cols, *befores)


def shards(integrals, occ_bins, vir_bins):
    nz, nh, nl, ny = (lax.axis_size(k) for k in ("z", "h", "l", "y"))
    z, h, l, y, c = (lax.axis_index(k) for k in ("z", "h", "l", "y", "c"))
    nj, slab, part = integrals.shape
    depth = nz * nh * part
    own = integrals.astype(jnp.bfloat16).reshape(nz, nh, slab, part)
    even, odd = own[:, 0], own[:, 1]
    first = h == 0
    mine = jnp.where(first, even, odd)
    sent = jnp.where(first, odd, even)
    sent = jnp.concatenate([sent[: nz // 2], sent[nz // 2 :]], axis=2)
    there = lax.ppermute(sent, "h", SWAP)
    there = jnp.concatenate([there[:, :, :part], there[:, :, part:]], axis=0)
    wide = jnp.concatenate([jnp.where(first, mine, there), jnp.where(first, there, mine)], axis=2)
    occupied = occupied_base - occupied_step * occ_bins.astype(jnp.float32)
    virtual = virtual_base + virtual_step * vir_bins.astype(jnp.float32)
    virtual = virtual.reshape(nl, ny, 2, slab)
    core0, low0 = c == 0, l == 0
    of_cols = lax.dynamic_slice_in_dim(virtual, y, 1, 1)[:, 0]
    of_cols = jnp.where(core0, of_cols[:, 0], of_cols[:, 1])
    low_own = jnp.where(low0, of_cols[0], of_cols[1])
    low_other = jnp.where(low0, of_cols[1], of_cols[0])
    evens, odds = occupied[0::2], occupied[1::2]

    def col_e(low, is_even):
        return (low[None, :] - jnp.where(is_even, evens, odds)[:, None]).reshape(1, -1)

    near_even = (h != l) == core0
    most_e = [col_e(low_own, h == 0), col_e(low_other, near_even), col_e(low_other, ~near_even)]
    rest_e = col_e(low_own, h != 0)
    wide, most_e, rest_e = lax.optimization_barrier((wide, jnp.concatenate(most_e, axis=1), rest_e))
    here = lax.all_gather(wide.reshape(nz * slab, nh * part), "z", axis=0, tiled=False)

    def shift(block, by):
        count = nh * nl
        ring = [(2 * k, 2 * ((k + by) % count)) for k in range(count)]
        ring += [(2 * k + 1, 2 * ((k - by) % count) + 1) for k in range(count)]
        return lax.ppermute(block, ("h", "l", "c"), ring)

    near, off = shift(here, 1), shift(here, -1)
    near, off = lax.optimization_barrier((near, off))
    far = shift(near, 1)
    seeds = lax.dynamic_slice_in_dim(here, z * slab, slab, 1)
    seeds = jnp.transpose(seeds, (1, 0, 2)).reshape(slab, depth)
    rows = lax.all_to_all(jnp.broadcast_to(seeds[None], (ny, slab, depth)), "y", 0, 0)
    rows = rows.reshape(ny * slab, depth)
    rows, virtual, occupied = lax.optimization_barrier((rows, virtual, occupied))
    rows_there = lax.ppermute(rows, "c", SWAP)
    occ_own = lax.dynamic_slice_in_dim(occupied, z * nh + h, 1, 0)
    of_rows = jnp.where(low0, virtual[0], virtual[1]) - occ_own
    own_e = jnp.where(core0, of_rows[:, 0], of_rows[:, 1]).reshape(-1, 1)
    there_e = jnp.where(core0, of_rows[:, 1], of_rows[:, 0]).reshape(-1, 1)

    f32, bf16 = jnp.float32, jnp.bfloat16
    both, both_e = [rows_there, rows], [there_e, own_e]
    work = 8 * rest_e.size * rows.size
    most = run((f32, f32), 1024, both, both_e, most_e, [here, near, off])
    for_there, for_own = run((bf16, f32), work, both, both_e, rest_e, [far], most)
    arrived = lax.ppermute(for_there, "c", SWAP)
    pair_sum = (for_own + arrived.astype(jnp.float32)).astype(jnp.bfloat16)
    shares = lax.all_to_all(pair_sum.reshape(ny, slab, depth), "y", 0, 0)
    density = jnp.sum(shares.astype(jnp.float32), axis=0)
    return density[:, None, :]


def solution(mesh):
    fine = Mesh(mesh.devices.reshape(12, 2, 2, 8, 2), ("z", "h", "l", "y", "c"))
    in_specs = (P(None, ("l", "y", "c"), ("z", "h")), P(), P())
    out_specs = P(("l", "y", "c"), ("z", "h"), None)
    return jax.shard_map(shards, mesh=fine, in_specs=in_specs, out_specs=out_specs, check_vma=False)
```

```python
import jax
import jax.numpy as jnp
from jax import lax
from jax.experimental import pallas as pl
from jax.experimental.pallas import tpu as pltpu
from jax.sharding import Mesh, PartitionSpec as P

occupied_base = -0.4
occupied_step = 0.01
virtual_base = 0.1
virtual_step = 0.01
spin_scale = 1.3

SWAP = [(0, 1), (1, 0)]


def density_kernel(sides, blocks, more, col_e, *refs):
    rows_refs, refs = refs[:sides], refs[sides:]
    row_es, refs = refs[:sides], refs[sides:]
    cols_refs, refs = refs[:blocks], refs[blocks:]
    befores, refs = (refs[:sides], refs[sides:]) if more else ([None] * sides, refs)
    outs, (full, sem) = refs[:sides], refs[sides:]
    copies, first, left = [], 0, 0
    for cols_ref in cols_refs:
        chunks, width, lanes = cols_ref.shape
        for k in range(chunks):
            there = full.at[pl.ds(first, width), pl.ds(left, lanes)]
            copies.append(pltpu.make_async_copy(cols_ref.at[k], there, sem.at[len(copies)]))
            left += lanes
        if left == full.shape[1]:
            first, left = first + width, 0
    for copy in copies:
        copy.start()
    rows = jnp.concatenate([ref[...] for ref in rows_refs], axis=0)
    row_e = jnp.concatenate([ref[...] for ref in row_es], axis=0)
    lanes = cols_refs[0].shape[2]
    middle = full.shape[1] // lanes // 2 * lanes
    starts = [k % (full.shape[1] // lanes) * lanes for k in range(len(copies))]
    pair = None
    for low, high in ((0, middle), (middle, full.shape[1])):
        for copy, start in zip(copies, starts):
            if low <= start < high:
                copy.wait()
        part = lax.dot_general(
            rows[:, low:high],
            full[:, low:high],
            (((1,), (1,)), ((), ())),
            preferred_element_type=jnp.float32,
        )
        pair = part if pair is None else pair + part
    amplitude = (spin_scale * pair / (row_e + col_e[...])).astype(jnp.bfloat16)
    terms = jnp.dot(amplitude, full[...], preferred_element_type=jnp.float32)
    count = outs[0].shape[0]
    for k, (before_ref, out_ref) in enumerate(zip(befores, outs)):
        term = terms[k * count : (k + 1) * count]
        if more:
            term = term + before_ref[...]
        out_ref[...] = term.astype(out_ref.dtype)


def run(kinds, work, rows, row_es, col_e, cols, befores=()):
    vmem = pl.BlockSpec(memory_space=pltpu.VMEM)
    anywhere = pl.BlockSpec(memory_space=pl.ANY)
    sides, blocks = len(rows), len(cols)
    return pl.pallas_call(
        lambda *refs: density_kernel(sides, blocks, len(befores) > 0, *refs),
        out_shape=[jax.ShapeDtypeStruct(side.shape, kind) for side, kind in zip(rows, kinds)],
        in_specs=[vmem] * (1 + 2 * sides) + [anywhere] * blocks + [vmem] * len(befores),
        out_specs=[vmem] * sides,
        scratch_shapes=[
            pltpu.VMEM((col_e.shape[1], rows[0].shape[1]), jnp.bfloat16),
            pltpu.SemaphoreType.DMA((sum(block.shape[0] for block in cols),)),
        ],
        compiler_params=pltpu.CompilerParams(vmem_limit_bytes=14 * 1024 * 1024),
        cost_estimate=pl.CostEstimate(flops=work, bytes_accessed=work // 256, transcendentals=0),
    )(col_e, *rows, *row_es, *cols, *befores)


def shards(integrals, occ_bins, vir_bins):
    nz, nh, nl, ny = (lax.axis_size(k) for k in ("z", "h", "l", "y"))
    z, h, l, y, c = (lax.axis_index(k) for k in ("z", "h", "l", "y", "c"))
    nj, slab, part = integrals.shape
    depth = nz * nh * part
    own = integrals.astype(jnp.bfloat16).reshape(nz, nh, slab, part)
    even, odd = own[:, 0], own[:, 1]
    first = h == 0
    mine = jnp.where(first, even, odd)
    sent = jnp.where(first, odd, even)
    sent = jnp.concatenate([sent[: nz // 2], sent[nz // 2 :]], axis=2)
    there = lax.ppermute(sent, "h", SWAP)
    there = jnp.concatenate([there[:, :, :part], there[:, :, part:]], axis=0)
    wide = jnp.concatenate([jnp.where(first, mine, there), jnp.where(first, there, mine)], axis=2)
    occupied = occupied_base - occupied_step * occ_bins.astype(jnp.float32)
    virtual = virtual_base + virtual_step * vir_bins.astype(jnp.float32)
    virtual = virtual.reshape(nl, ny, 2, slab)
    core0, low0 = c == 0, l == 0
    of_cols = lax.dynamic_slice_in_dim(virtual, y, 1, 1)[:, 0]
    of_cols = jnp.where(core0, of_cols[:, 0], of_cols[:, 1])
    low_own = jnp.where(low0, of_cols[0], of_cols[1])
    low_other = jnp.where(low0, of_cols[1], of_cols[0])
    evens, odds = occupied[0::2], occupied[1::2]

    def col_e(low, is_even):
        return (low[None, :] - jnp.where(is_even, evens, odds)[:, None]).reshape(1, -1)

    near_even = (h != l) == core0
    most_e = [col_e(low_own, h == 0), col_e(low_other, near_even), col_e(low_other, ~near_even)]
    rest_e = col_e(low_own, h != 0)
    wide, most_e, rest_e = lax.optimization_barrier((wide, jnp.concatenate(most_e, axis=1), rest_e))
    here = lax.all_gather(wide.reshape(nz * slab, nh * part), "z", axis=0, tiled=False)

    def shift(block, by):
        count = nh * nl
        ring = [(2 * k, 2 * ((k + by) % count)) for k in range(count)]
        ring += [(2 * k + 1, 2 * ((k - by) % count) + 1) for k in range(count)]
        return lax.ppermute(block, ("h", "l", "c"), ring)

    near, off = shift(here, 1), shift(here, -1)
    near, off = lax.optimization_barrier((near, off))
    far = shift(near, 1)
    seeds = lax.dynamic_slice_in_dim(here, z * slab, slab, 1)
    seeds = jnp.transpose(seeds, (1, 0, 2)).reshape(slab, depth)
    rows = lax.all_to_all(jnp.broadcast_to(seeds[None], (ny, slab, depth)), "y", 0, 0)
    rows = rows.reshape(ny * slab, depth)
    rows, virtual, occupied = lax.optimization_barrier((rows, virtual, occupied))
    rows_there = lax.ppermute(rows, "c", SWAP)
    occ_own = lax.dynamic_slice_in_dim(occupied, z * nh + h, 1, 0)
    of_rows = jnp.where(low0, virtual[0], virtual[1]) - occ_own
    own_e = jnp.where(core0, of_rows[:, 0], of_rows[:, 1]).reshape(-1, 1)
    there_e = jnp.where(core0, of_rows[:, 1], of_rows[:, 0]).reshape(-1, 1)

    f32, bf16 = jnp.float32, jnp.bfloat16
    both, both_e = [rows_there, rows], [there_e, own_e]
    work = 8 * rest_e.size * rows.size
    most = run((f32, f32), 1024, both, both_e, most_e, [here, near, off])
    for_there, for_own = run((bf16, f32), work, both, both_e, rest_e, [far], most)
    arrived = lax.ppermute(for_there, "c", SWAP)
    pair_sum = (for_own + arrived.astype(jnp.float32)).astype(jnp.bfloat16)
    shares = lax.all_to_all(pair_sum.reshape(ny, slab, depth), "y", 0, 0)
    def add_kernel(shares_ref, out_ref):
        total = shares_ref[0].astype(jnp.float32)
        for k in range(1, shares_ref.shape[0]):
            total = total + shares_ref[k].astype(jnp.float32)
        out_ref[...] = total[:, None, :]

    vmem = pl.BlockSpec(memory_space=pltpu.VMEM)
    return pl.pallas_call(
        add_kernel,
        out_shape=jax.ShapeDtypeStruct((slab, 1, depth), jnp.float32),
        in_specs=[vmem],
        out_specs=vmem,
    )(shares)


def solution(mesh):
    fine = Mesh(mesh.devices.reshape(12, 2, 2, 8, 2), ("z", "h", "l", "y", "c"))
    in_specs = (P(None, ("l", "y", "c"), ("z", "h")), P(), P())
    out_specs = P(("l", "y", "c"), ("z", "h"), None)
    return jax.shard_map(shards, mesh=fine, in_specs=in_specs, out_specs=out_specs, check_vma=False)
```
